256 devices in a mesh: tm: 8 (over z_lo, y), space: 32 (over z_hi, x, core).
Axes of the slice: x: 4, y: 4, z: 8 (z_hi: 4, z_lo: 2; z = z_hi * 2 + z_lo), core: 2. Of those that a mesh axis runs over, the one named last changes fastest.
Arguments:
- coupling: float32 [448, 65536], P(None, 'space'), may hold values from -0.02734375 to 0.02734375
- retain: float32 [65536], P('space'), may hold values from 0.5 to 0.92
- sources: float32 [96, 65536], P('tm', 'space'), may hold values from -1.5 to 1.5
- initial_guess: float32 [24, 65536], P('tm', 'space'), may hold values from -5 to 5
- start_field: float32 [65536], P('space'), may hold values from -5 to 5
- block_columns: int32 [1024, 6], P('space'), may hold values from 0 to 63
- send_lists: int32 [64, 16], P('space'), may hold values from 0 to 31, as said below
Outputs:
- point_values: float32 [24, 65536], P('tm', 'space')
- residual: float32 [24, 65536], P('tm', 'space')
The draws below stay inside these ranges and needn't reach their ends.
Inputs may be any that keep to these rules, and one draw needn't show every extreme that they name: `block_columns`: entries are numbers in the extended list of the block's own space index: own blocks first, then the 16 blocks received from the lower neighbour, then the 16 from the upper one. `send_lists`: row 2 s lists the blocks that space index s sends to index s - 1, row 2 s + 1 those it sends to index s + 1, numbered within index s; the 16 entries of a row are distinct.
All inputs are finite; a program needn't handle non-finite values.
Results may differ from the reference program's by a relative error of at most 0.00015.
Values sent between devices are 32-bit elements; how exact they have to be, the bound alone decides.
A program may use at most 64 MiB of HBM per device.

```python
import jax
import jax.numpy as jnp
from jax import lax

BS = 64
STENCIL = 7
NBLK = 32
CF = 4
PASSES = 2
HALO = 16
NC = 24
NT = 96
BLOCKS = 1024
CELLS = 65536
SEND_LISTS = 64
N_SPACE = 32


def draw_send_lists(key, part):
    keys = jax.random.split(key, SEND_LISTS)

    def one_order(one_key):
        return jax.random.permutation(one_key, NBLK)
    orders = jax.vmap(one_order)(keys)
    return orders[:, :HALO].astype(jnp.int32)


def plant(entries, rng, low, largest):
    index_at = [jax.random.randint(jax.random.fold_in(rng, axis), (), 0, length) for axis, length in enumerate(entries.shape)]
    main_axis = entries.shape.index(max(entries.shape))
    beside = index_at[:main_axis] + [(index_at[main_axis] + 1) % entries.shape[main_axis]] + index_at[main_axis + 1:]
    return entries.at[tuple(index_at)].set(low).at[tuple(beside)].set(largest)


def level_of(rng, extent, shards, least, largest):
    factor_of, own = 1.0, jax.random.fold_in(rng, 6)
    for axis_at, parts in shards:
        draws = jnp.exp(jax.random.uniform(jax.random.fold_in(own, axis_at), (parts,), jnp.float32, least / len(shards), largest / len(shards)))
        factor_of = factor_of * jnp.repeat(draws, extent[axis_at] // parts).reshape([-1 if axis == axis_at else 1 for axis in range(len(extent))])
    return factor_of


def noise(own_key, dims, deviation, reach, pieces=(), kind=jnp.bfloat16):
    level = level_of(own_key, dims, pieces, -0.22, 0.18) if pieces else 1.0
    entries = jax.random.normal(own_key, dims, jnp.float32) * deviation * level
    return jnp.minimum(jnp.maximum(entries, -reach), reach).astype(kind)


def setup_inputs(seed: int = 0) -> dict:
    key_list = jax.random.split(jax.random.key(seed), 8)
    coupling = noise(key_list[0], (STENCIL * BS, CELLS), (100 * STENCIL * BS) ** -0.5, 0.02734375, ((1, 32),), jnp.float32)
    retain = jnp.clip(0.5 + 0.42000002 * jax.random.uniform(key_list[1], (CELLS,), jnp.float32) ** level_of(key_list[1], (CELLS,), ((0, 32),), -0.2, 0.2), 0.5, 0.92)
    sources = noise(key_list[2], (NT, CELLS), 0.25, 1.5, ((0, 8), (1, 32)), jnp.float32)
    initial_guess = noise(key_list[3], (NC, CELLS), 1.0, 5.0, ((0, 8), (1, 32)), jnp.float32)
    start_field = noise(key_list[4], (CELLS,), 1.0, 5.0, ((0, 32),), jnp.float32)
    block_columns = plant(jax.random.randint(key_list[5], (BLOCKS, STENCIL - 1), 0, NBLK + 2 * HALO), jax.random.fold_in(key_list[5], 1), 0, (NBLK + 2 * HALO) - 1).astype(jnp.int32)
    send_lists = draw_send_lists(jax.random.fold_in(key_list[7], 71), 0)
    return {"coupling": coupling, "retain": retain, "sources": sources, "initial_guess": initial_guess, "start_field": start_field, "block_columns": block_columns, "send_lists": send_lists}


def pick_blocks(shard_blocks, shard_list):
    return shard_blocks[:, shard_list, :]


def neighbour_term(field_now, coupling, columns, send_lists):
    count_rows = field_now.shape[0]
    blocks = field_now.reshape(count_rows, N_SPACE, NBLK, BS)
    lists = send_lists.reshape(N_SPACE, 2, HALO)
    to_lower = jax.vmap(pick_blocks, in_axes=(1, 0), out_axes=1)(blocks, lists[:, 0])
    to_upper = jax.vmap(pick_blocks, in_axes=(1, 0), out_axes=1)(blocks, lists[:, 1])
    empty = jnp.zeros((count_rows, 1, HALO, BS), field_now.dtype)
    from_lower = jnp.concatenate([empty, to_upper[:, :-1]], axis=1)
    from_upper = jnp.concatenate([to_lower[:, 1:], empty], axis=1)
    extended = jnp.concatenate([blocks, from_lower, from_upper], axis=2)

    def gather_shard(shard_ext, shard_cols):
        return shard_ext[:, shard_cols, :].reshape(count_rows, NBLK, STENCIL * BS)

    picked = jax.vmap(gather_shard, in_axes=(1, 0), out_axes=1)(extended, columns)
    weights = coupling.reshape(STENCIL * BS, N_SPACE, NBLK, BS)
    result = jnp.einsum("rsbi,isbc->rsbc", picked, weights, precision=lax.Precision.HIGHEST)
    return result.reshape(count_rows, CELLS)


def reference(coupling, retain, sources, initial_guess, start_field, block_columns, send_lists):
    own_blocks = jnp.broadcast_to(jnp.arange(NBLK, dtype=jnp.int32)[None, :, None], (N_SPACE, NBLK, 1))
    columns = jnp.concatenate([own_blocks, block_columns.reshape(N_SPACE, NBLK, STENCIL - 1).astype(jnp.int32)], axis=2)
    forcing = sources.reshape(NC, CF, CELLS)

    def propagate(starting):
        field_now = starting
        for section in range(CF):
            field_now = retain[None] * field_now + neighbour_term(field_now, coupling, columns, send_lists) + forcing[:, section]
        return field_now

    values = initial_guess
    for sweep_index in range(2 * PASSES):
        values = propagate(jnp.concatenate([start_field[None], values[:-1]], axis=0))
    residual = propagate(jnp.concatenate([start_field[None], values[:-1]], axis=0)) - values
    return (values, residual)
```

```python
import functools

import jax
import jax.numpy as jnp
from jax import lax
from jax.experimental import pallas as pl
from jax.experimental.pallas import tpu as pltpu
from jax.sharding import PartitionSpec as P

BS = 64
STENCIL = 7
NBLK = 32
CF = 4
C_DEV = 3
SWEEPS = 5
HALO = 16
PAIRS = NBLK // 2
GROUPS = NBLK // 4
STEPS = SWEEPS * CF
REST = (STENCIL - 1) * BS
MESH = pl.DeviceIdType.MESH


def kernel(
    n_tm,
    n_space,
    columns,
    lists,
    coupling_hbm,
    retain,
    sources,
    guess,
    start,
    values_out,
    residual_out,
    coupling,
    own_weights,
    weights,
    forcing,
    guess_out,
    guess_in,
    retained,
    state,
    reached,
    doubled,
    parts,
    base,
    outbox,
    inbox,
    point_out,
    point_in,
    coupling_sem,
    send_sem,
    recv_sem,
    slice_send,
    slice_recv,
):
    tm, space = lax.axis_index("tm"), lax.axis_index("space")
    before = [lax.rem(tm + n_tm - d, n_tm) for d in range(3)]
    after = [lax.rem(tm + d, n_tm) for d in range(3)]
    has = (space > 0, space < n_space - 1)
    beside = (space - 1, space + 1)

    lane = lax.broadcasted_iota(jnp.int32, (8, 128), 1)
    row = lax.broadcasted_iota(jnp.int32, (8, 128), 0)
    low, top = lane < BS, row < 4
    field = lax.rem(row, 4)

    loads = [
        pltpu.make_async_copy(
            coupling_hbm.at[pl.ds(BS * k, BS), :], coupling.at[pl.ds(BS * k, BS), :], coupling_sem.at[k]
        )
        for k in range(STENCIL)
    ]
    for load in loads:
        load.start()

    def cells(p):
        return pl.ds(128 * p, 128)

    inbox[...] = jnp.zeros_like(inbox)
    for p in range(PAIRS):
        for f in range(C_DEV):
            guess_out[pl.ds(16 * f + p, 1), :] = guess[pl.ds(f, 1), cells(p)]
            forcing[pl.ds(64 * (4 + f) + 4 * p, 4), :] = sources[pl.ds(4 * f, 4), cells(p)]
    forcing[pl.ds(448, 64), :] = jnp.zeros((64, 128), jnp.float32)

    barrier = pltpu.get_barrier_semaphore()
    for other in (before[1], before[2], after[1], after[2]):
        pl.semaphore_signal(barrier, inc=1, device_id={"tm": other}, device_id_type=MESH)
    for side in range(2):

        @pl.when(has[side])
        def _():
            pl.semaphore_signal(barrier, inc=1, device_id={"space": beside[side]}, device_id_type=MESH)

    pl.semaphore_wait(barrier, 4 + has[0].astype(jnp.int32) + has[1].astype(jnp.int32))

    def to_slice(n, source, target, other):
        return pltpu.make_async_remote_copy(
            src_ref=source,
            dst_ref=target,
            send_sem=slice_send.at[n],
            recv_sem=slice_recv.at[n],
            device_id={"tm": other},
            device_id_type=MESH,
        )

    def interval(a):
        return forcing.at[pl.ds(64 * a, 64), :]

    slice_copies = [
        to_slice(0, guess_out.at[pl.ds(16, 32), :], guess_in.at[pl.ds(0, 32), :], after[2]),
        to_slice(1, guess_out.at[pl.ds(0, 16), :], guess_in.at[pl.ds(32, 16), :], after[1]),
        to_slice(2, interval(6), interval(0), after[2]),
        to_slice(3, interval(4), interval(1), after[1]),
        to_slice(4, interval(5), interval(2), after[1]),
        to_slice(5, interval(6), interval(3), after[1]),
    ]
    for copy in slice_copies:
        copy.start()
    point_copy = to_slice(6, point_out, point_in, before[1])

    def halo_copy(slot, side):
        return pltpu.make_async_remote_copy(
            src_ref=outbox.at[slot, side],
            dst_ref=inbox.at[slot, 1 - side],
            send_sem=send_sem.at[slot, side],
            recv_sem=recv_sem.at[slot, 1 - side],
            device_id={"space": beside[side]},
            device_id_type=MESH,
        )

    def twice(value):
        turned = pltpu.roll(value, BS, 1)
        return jnp.where(low, value, turned), jnp.where(low, turned, value)

    def in_parts(value):
        upper = value.astype(jnp.bfloat16).astype(jnp.float32)
        return jnp.where(top, upper, value - upper)

    def send(step, values):
        slot = lax.rem(step, 2)
        begins = jnp.where(lax.rem(step, CF) == 0, 4 - C_DEV * tm - step // CF, -1)
        for p in range(PAIRS):
            value = jnp.where(field == begins, start[pl.ds(p, 1), :], values[p])
            state[p] = value
            doubled[2 * p], doubled[2 * p + 1] = twice(value)
        for side in range(2):
            for q in range(HALO // 2):
                pair = jnp.where(low, doubled[lists[side, 2 * q]], doubled[lists[side, 2 * q + 1]])
                outbox[slot, side, pl.ds(4 * q, 4), :] = pair[:4]

            @pl.when(has[side])
            def _():
                halo_copy(slot, side).start()

    for copy in slice_copies[:2]:
        copy.wait_recv()
    first = []
    for p in range(PAIRS):
        rows = [guess_in[pl.ds(16 * f + p, 1), :] for f in range(C_DEV)]
        rows.append(jnp.zeros((1, 128), jnp.float32))
        first.append(jnp.concatenate(rows + rows, axis=0))
    send(jnp.int32(0), first)

    for p in range(PAIRS):
        retained[p] = jnp.where(top, retain[pl.ds(p, 1), :], 0.0)
    for k in range(STENCIL):
        loads[k].wait()
        target, at, gap = (own_weights, 0, BS) if k == 0 else (weights, BS * (k - 1), REST)

        @pl.loop(0, BS // 16)
        def _(n, k=k, target=target, at=at, gap=gap):
            entries = coupling[pl.ds(pl.multiple_of(BS * k + 16 * n, 16), 16), :]
            upper = entries.astype(jnp.bfloat16)
            target[pl.ds(pl.multiple_of(at + 16 * n, 16), 16), :] = upper
            target[pl.ds(pl.multiple_of(at + gap + 16 * n, 16), 16), :] = (
                entries - upper.astype(jnp.float32)
            ).astype(jnp.bfloat16)

    def on_diagonal(product):
        return [
            jnp.where(
                low,
                product[16 * h : 16 * h + 8, 128 * h : 128 * h + 128],
                product[16 * h + 8 : 16 * h + 16, 128 * h : 128 * h + 128],
            )
            for h in range(2)
        ]

    def one_step(step, carry):
        slot = lax.rem(step, 2)

        @pl.when(step == 0)
        def _():
            for copy in slice_copies[2:]:
                copy.wait_recv()

        @pl.when(step == 4 * CF)
        def _():
            for p in range(PAIRS):
                value = reached[p]
                values_out[pl.ds(0, 2), cells(p)] = value[1:3]
                point_out[pl.ds(p, 1), :] = value[0:1]
            point_copy.start()

        at = (step // CF) * 64 + lax.rem(step, CF)
        for g in range(GROUPS):
            own = []
            for b in range(4 * g, 4 * g + 4):
                own.append(in_parts(doubled[b]))
                parts[b] = own[-1]
            product = jnp.dot(
                jnp.concatenate(own, axis=0).astype(jnp.bfloat16),
                own_weights[:, 256 * g : 256 * g + 256],
                preferred_element_type=jnp.float32,
            )
            for h, pair in enumerate(on_diagonal(product)):
                p = 2 * g + h
                heat = forcing[pl.ds(at + 4 * p, 4, stride=64), :]
                heat = jnp.concatenate([heat, jnp.zeros((4, 128), jnp.float32)], axis=0)
                base[p] = pair + retained[p] * state[p] + heat

        for side in range(2):

            @pl.when(has[side])
            def _():
                halo_copy(slot, 1 - side).wait_recv()

        for side in range(2):
            for q in range(HALO // 2):
                value = inbox[slot, side, pl.ds(4 * q, 4), :]
                both = twice(in_parts(jnp.concatenate([value, value], axis=0)))
                n = NBLK + HALO * side + 2 * q
                parts[n], parts[n + 1] = both

        values = []
        for g in range(GROUPS):
            picked = []
            for b in range(4 * g, 4 * g + 4):
                picked.append(
                    jnp.concatenate(
                        [
                            jnp.where(low, parts[columns[b, k]], parts[columns[b, k + 1]])
                            for k in range(0, STENCIL - 1, 2)
                        ],
                        axis=1,
                    )
                )
            left = jnp.concatenate(picked, axis=0).astype(jnp.bfloat16)
            product = jnp.dot(
                jnp.concatenate([left, left], axis=1),
                weights[:, 256 * g : 256 * g + 256],
                preferred_element_type=jnp.float32,
            )
            for h, pair in enumerate(on_diagonal(product)):
                total = base[2 * g + h] + pair
                values.append(total + pltpu.roll(total, 4, 0))
                reached[2 * g + h] = values[-1]

        for side in range(2):

            @pl.when(has[side])
            def _():
                halo_copy(slot, side).wait_send()

        @pl.when(step < STEPS - 1)
        def _():
            send(step + 1, [reached[p] for p in range(PAIRS)])

        return carry

    lax.fori_loop(0, STEPS, one_step, 0)

    for copy in slice_copies:
        copy.wait_send()
    point_copy.wait()
    for p in range(PAIRS):
        values_out[pl.ds(2, 1), cells(p)] = point_in[pl.ds(p, 1), :]
        residual_out[:, cells(p)] = reached[p][:3] - values_out[:, cells(p)]


def body(n_tm, n_space, coupling, retain, sources, initial_guess, start_field, block_columns, send_lists):
    count = retain.shape[0]
    f32, bf16 = jnp.float32, jnp.bfloat16
    smem, vmem = (pl.BlockSpec(memory_space=space) for space in (pltpu.SMEM, pltpu.VMEM))
    return pl.pallas_call(
        functools.partial(kernel, n_tm, n_space),
        out_shape=(jax.ShapeDtypeStruct((C_DEV, count), f32),) * 2,
        in_specs=[smem, smem, pl.BlockSpec(memory_space=pl.ANY), vmem, vmem, vmem, vmem],
        out_specs=(vmem, vmem),
        scratch_shapes=[
            pltpu.VMEM((STENCIL * BS, count), f32),
            pltpu.VMEM((2 * BS, count), bf16),
            pltpu.VMEM((2 * REST, count), bf16),
            pltpu.VMEM((512, 128), f32),
            pltpu.VMEM((48, 128), f32),
            pltpu.VMEM((48, 128), f32),
            pltpu.VMEM((PAIRS, 8, 128), f32),
            pltpu.VMEM((PAIRS, 8, 128), f32),
            pltpu.VMEM((PAIRS, 8, 128), f32),
            pltpu.VMEM((NBLK, 8, 128), f32),
            pltpu.VMEM((NBLK + 2 * HALO, 8, 128), f32),
            pltpu.VMEM((PAIRS, 8, 128), f32),
            pltpu.VMEM((2, 2, 32, 128), f32),
            pltpu.VMEM((2, 2, 32, 128), f32),
            pltpu.VMEM((16, 128), f32),
            pltpu.VMEM((16, 128), f32),
            pltpu.SemaphoreType.DMA((STENCIL,)),
            pltpu.SemaphoreType.DMA((2, 2)),
            pltpu.SemaphoreType.DMA((2, 2)),
            pltpu.SemaphoreType.DMA((7,)),
            pltpu.SemaphoreType.DMA((7,)),
        ],
        compiler_params=pltpu.CompilerParams(
            collective_id=0, has_side_effects=True, vmem_limit_bytes=32 * 2**20
        ),
    )(
        block_columns,
        send_lists,
        coupling,
        retain.reshape(PAIRS, 128),
        sources,
        initial_guess,
        start_field.reshape(PAIRS, 128),
    )


def solution(mesh):
    placed = (
        P(None, "space"),
        P("space"),
        P("tm", "space"),
        P("tm", "space"),
        P("space"),
        P("space", None),
        P("space", None),
    )
    return jax.shard_map(
        functools.partial(body, mesh.shape["tm"], mesh.shape["space"]),
        mesh=mesh,
        in_specs=placed,
        out_specs=(P("tm", "space"), P("tm", "space")),
        check_vma=False,
    )
```

```python
import functools

import jax
import jax.numpy as jnp
from jax import lax
from jax.experimental import pallas as pl
from jax.experimental.pallas import tpu as pltpu
from jax.sharding import PartitionSpec as P

BS = 64
STENCIL = 7
NBLK = 32
CF = 4
C_DEV = 3
SWEEPS = 5
HALO = 16
PAIRS = NBLK // 2
GROUPS = NBLK // 4
STEPS = SWEEPS * CF
REST = (STENCIL - 1) * BS
MESH = pl.DeviceIdType.MESH


def kernel(
    n_tm,
    n_space,
    columns,
    lists,
    coupling_hbm,
    retain_hbm,
    sources_hbm,
    guess_hbm,
    start_hbm,
    values_out,
    residual_out,
    retain,
    sources,
    guess,
    start,
    coupling,
    own_weights,
    weights,
    forcing,
    guess_out,
    guess_in,
    retained,
    state,
    reached,
    doubled,
    parts,
    base,
    outbox,
    inbox,
    point_out,
    point_in,
    coupling_sem,
    input_sem,
    send_sem,
    recv_sem,
    slice_send,
    slice_recv,
):
    tm, space = lax.axis_index("tm"), lax.axis_index("space")
    before = [lax.rem(tm + n_tm - d, n_tm) for d in range(3)]
    after = [lax.rem(tm + d, n_tm) for d in range(3)]
    has = (space > 0, space < n_space - 1)
    beside = (space - 1, space + 1)

    lane = lax.broadcasted_iota(jnp.int32, (8, 128), 1)
    row = lax.broadcasted_iota(jnp.int32, (8, 128), 0)
    low, top = lane < BS, row < 4
    field = lax.rem(row, 4)

    loads = [
        pltpu.make_async_copy(
            coupling_hbm.at[pl.ds(BS * k, BS), :], coupling.at[pl.ds(BS * k, BS), :], coupling_sem.at[k]
        )
        for k in range(STENCIL)
    ]
    inputs = [
        pltpu.make_async_copy(source, target, input_sem.at[n])
        for n, (source, target) in enumerate(
            ((guess_hbm, guess), (sources_hbm, sources), (start_hbm, start), (retain_hbm, retain))
        )
    ]
    for load in inputs + loads:
        load.start()

    def cells(p):
        return pl.ds(128 * p, 128)

    inbox[...] = jnp.zeros_like(inbox)
    barrier = pltpu.get_barrier_semaphore()
    for other in (before[1], before[2], after[1], after[2]):
        pl.semaphore_signal(barrier, inc=1, device_id={"tm": other}, device_id_type=MESH)
    for side in range(2):

        @pl.when(has[side])
        def _():
            pl.semaphore_signal(barrier, inc=1, device_id={"space": beside[side]}, device_id_type=MESH)

    for load in inputs[:2]:
        load.wait()
    for p in range(PAIRS):
        for f in range(C_DEV):
            guess_out[pl.ds(16 * f + p, 1), :] = guess[pl.ds(f, 1), cells(p)]
            forcing[pl.ds(64 * (4 + f) + 4 * p, 4), :] = sources[pl.ds(4 * f, 4), cells(p)]
    forcing[pl.ds(448, 64), :] = jnp.zeros((64, 128), jnp.float32)

    pl.semaphore_wait(barrier, 4 + has[0].astype(jnp.int32) + has[1].astype(jnp.int32))

    def to_slice(n, source, target, other):
        return pltpu.make_async_remote_copy(
            src_ref=source,
            dst_ref=target,
            send_sem=slice_send.at[n],
            recv_sem=slice_recv.at[n],
            device_id={"tm": other},
            device_id_type=MESH,
        )

    def interval(a):
        return forcing.at[pl.ds(64 * a, 64), :]

    slice_copies = [
        to_slice(0, guess_out.at[pl.ds(16, 32), :], guess_in.at[pl.ds(0, 32), :], after[2]),
        to_slice(1, guess_out.at[pl.ds(0, 16), :], guess_in.at[pl.ds(32, 16), :], after[1]),
        to_slice(2, interval(6), interval(0), after[2]),
        to_slice(3, interval(4), interval(1), after[1]),
        to_slice(4, interval(5), interval(2), after[1]),
        to_slice(5, interval(6), interval(3), after[1]),
    ]
    for copy in slice_copies:
        copy.start()
    point_copy = to_slice(6, point_out, point_in, before[1])

    def halo_copy(slot, side):
        return pltpu.make_async_remote_copy(
            src_ref=outbox.at[slot, side],
            dst_ref=inbox.at[slot, 1 - side],
            send_sem=send_sem.at[slot, side],
            recv_sem=recv_sem.at[slot, 1 - side],
            device_id={"space": beside[side]},
            device_id_type=MESH,
        )

    def twice(value):
        turned = pltpu.roll(value, BS, 1)
        return jnp.where(low, value, turned), jnp.where(low, turned, value)

    def in_parts(value):
        upper = value.astype(jnp.bfloat16).astype(jnp.float32)
        return jnp.where(top, upper, value - upper)

    def send(step, values):
        slot = lax.rem(step, 2)
        begins = jnp.where(lax.rem(step, CF) == 0, 4 - C_DEV * tm - step // CF, -1)
        for p in range(PAIRS):
            value = jnp.where(field == begins, start[pl.ds(p, 1), :], values[p])
            state[p] = value
            doubled[2 * p], doubled[2 * p + 1] = twice(value)
        for side in range(2):
            for q in range(HALO // 2):
                pair = jnp.where(low, doubled[lists[side, 2 * q]], doubled[lists[side, 2 * q + 1]])
                outbox[slot, side, pl.ds(4 * q, 4), :] = pair[:4]

            @pl.when(has[side])
            def _():
                halo_copy(slot, side).start()

    for copy in slice_copies[:2]:
        copy.wait_recv()
    inputs[2].wait()
    first = []
    for p in range(PAIRS):
        rows = [guess_in[pl.ds(16 * f + p, 1), :] for f in range(C_DEV)]
        rows.append(jnp.zeros((1, 128), jnp.float32))
        first.append(jnp.concatenate(rows + rows, axis=0))
    send(jnp.int32(0), first)

    inputs[3].wait()
    for p in range(PAIRS):
        retained[p] = jnp.where(top, retain[pl.ds(p, 1), :], 0.0)
    for k in range(STENCIL):
        loads[k].wait()
        target, at, gap = (own_weights, 0, BS) if k == 0 else (weights, BS * (k - 1), REST)

        @pl.loop(0, BS // 16)
        def _(n, k=k, target=target, at=at, gap=gap):
            entries = coupling[pl.ds(pl.multiple_of(BS * k + 16 * n, 16), 16), :]
            upper = entries.astype(jnp.bfloat16)
            target[pl.ds(pl.multiple_of(at + 16 * n, 16), 16), :] = upper
            target[pl.ds(pl.multiple_of(at + gap + 16 * n, 16), 16), :] = (
                entries - upper.astype(jnp.float32)
            ).astype(jnp.bfloat16)

    def on_diagonal(product):
        return [
            jnp.where(
                low,
                product[16 * h : 16 * h + 8, 128 * h : 128 * h + 128],
                product[16 * h + 8 : 16 * h + 16, 128 * h : 128 * h + 128],
            )
            for h in range(2)
        ]

    def one_step(step, carry):
        slot = lax.rem(step, 2)

        @pl.when(step == 0)
        def _():
            for copy in slice_copies[2:]:
                copy.wait_recv()

        @pl.when(step == 4 * CF)
        def _():
            for p in range(PAIRS):
                value = reached[p]
                values_out[pl.ds(0, 2), cells(p)] = value[1:3]
                point_out[pl.ds(p, 1), :] = value[0:1]
            point_copy.start()

        at = (step // CF) * 64 + lax.rem(step, CF)
        for g in range(GROUPS):
            own = []
            for b in range(4 * g, 4 * g + 4):
                own.append(in_parts(doubled[b]))
                parts[b] = own[-1]
            product = jnp.dot(
                jnp.concatenate(own, axis=0).astype(jnp.bfloat16),
                own_weights[:, 256 * g : 256 * g + 256],
                preferred_element_type=jnp.float32,
            )
            for h, pair in enumerate(on_diagonal(product)):
                p = 2 * g + h
                heat = forcing[pl.ds(at + 4 * p, 4, stride=64), :]
                heat = jnp.concatenate([heat, jnp.zeros((4, 128), jnp.float32)], axis=0)
                base[p] = pair + retained[p] * state[p] + heat

        for side in range(2):

            @pl.when(has[side])
            def _():
                halo_copy(slot, 1 - side).wait_recv()

        for side in range(2):
            for q in range(HALO // 2):
                value = inbox[slot, side, pl.ds(4 * q, 4), :]
                both = twice(in_parts(jnp.concatenate([value, value], axis=0)))
                n = NBLK + HALO * side + 2 * q
                parts[n], parts[n + 1] = both

        values = []
        for g in range(GROUPS):
            picked = []
            for b in range(4 * g, 4 * g + 4):
                picked.append(
                    jnp.concatenate(
                        [
                            jnp.where(low, parts[columns[k, b]], parts[columns[k + 1, b]])
                            for k in range(0, STENCIL - 1, 2)
                        ],
                        axis=1,
                    )
                )
            left = jnp.concatenate(picked, axis=0).astype(jnp.bfloat16)
            product = jnp.dot(
                jnp.concatenate([left, left], axis=1),
                weights[:, 256 * g : 256 * g + 256],
                preferred_element_type=jnp.float32,
            )
            for h, pair in enumerate(on_diagonal(product)):
                total = base[2 * g + h] + pair
                values.append(total + pltpu.roll(total, 4, 0))
                reached[2 * g + h] = values[-1]

        for side in range(2):

            @pl.when(has[side])
            def _():
                halo_copy(slot, side).wait_send()

        @pl.when(step < STEPS - 1)
        def _():
            send(step + 1, [reached[p] for p in range(PAIRS)])

        return carry

    lax.fori_loop(0, STEPS, one_step, 0)

    for copy in slice_copies:
        copy.wait_send()
    point_copy.wait()
    for p in range(PAIRS):
        values_out[pl.ds(2, 1), cells(p)] = point_in[pl.ds(p, 1), :]
        residual_out[:, cells(p)] = reached[p][:3] - values_out[:, cells(p)]


def body(n_tm, n_space, coupling, retain, sources, initial_guess, start_field, block_columns, send_lists):
    count = retain.shape[0]
    f32, bf16 = jnp.float32, jnp.bfloat16
    smem, vmem = (pl.BlockSpec(memory_space=space) for space in (pltpu.SMEM, pltpu.VMEM))
    return pl.pallas_call(
        functools.partial(kernel, n_tm, n_space),
        out_shape=(jax.ShapeDtypeStruct((C_DEV, count), f32),) * 2,
        in_specs=[smem, smem] + [pl.BlockSpec(memory_space=pl.ANY)] * 5,
        out_specs=(vmem, vmem),
        scratch_shapes=[
            pltpu.VMEM((PAIRS, 128), f32),
            pltpu.VMEM((C_DEV * CF, count), f32),
            pltpu.VMEM((C_DEV, count), f32),
            pltpu.VMEM((PAIRS, 128), f32),
            pltpu.VMEM((STENCIL * BS, count), f32),
            pltpu.VMEM((2 * BS, count), bf16),
            pltpu.VMEM((2 * REST, count), bf16),
            pltpu.VMEM((512, 128), f32),
            pltpu.VMEM((48, 128), f32),
            pltpu.VMEM((48, 128), f32),
            pltpu.VMEM((PAIRS, 8, 128), f32),
            pltpu.VMEM((PAIRS, 8, 128), f32),
            pltpu.VMEM((PAIRS, 8, 128), f32),
            pltpu.VMEM((NBLK, 8, 128), f32),
            pltpu.VMEM((NBLK + 2 * HALO, 8, 128), f32),
            pltpu.VMEM((PAIRS, 8, 128), f32),
            pltpu.VMEM((2, 2, 32, 128), f32),
            pltpu.VMEM((2, 2, 32, 128), f32),
            pltpu.VMEM((16, 128), f32),
            pltpu.VMEM((16, 128), f32),
            pltpu.SemaphoreType.DMA((STENCIL,)),
            pltpu.SemaphoreType.DMA((4,)),
            pltpu.SemaphoreType.DMA((2, 2)),
            pltpu.SemaphoreType.DMA((2, 2)),
            pltpu.SemaphoreType.DMA((7,)),
            pltpu.SemaphoreType.DMA((7,)),
        ],
        compiler_params=pltpu.CompilerParams(
            collective_id=0, has_side_effects=True, vmem_limit_bytes=60 * 2**20
        ),
    )(
        block_columns.T,
        send_lists,
        coupling,
        retain.reshape(PAIRS, 128),
        sources,
        initial_guess,
        start_field.reshape(PAIRS, 128),
    )


def solution(mesh):
    placed = (
        P(None, "space"),
        P("space"),
        P("tm", "space"),
        P("tm", "space"),
        P("space"),
        P("space", None),
        P("space", None),
    )
    return jax.shard_map(
        functools.partial(body, mesh.shape["tm"], mesh.shape["space"]),
        mesh=mesh,
        in_specs=placed,
        out_specs=(P("tm", "space"), P("tm", "space")),
        check_vma=False,
    )
```

```python
import functools

import jax
import jax.numpy as jnp
from jax import lax
from jax.experimental import pallas as pl
from jax.experimental.pallas import tpu as pltpu
from jax.sharding import PartitionSpec as P

BS = 64
STENCIL = 7
NBLK = 32
CF = 4
C_DEV = 3
SWEEPS = 5
HALO = 16
PAIRS = NBLK // 2
GROUPS = NBLK // 4
STEPS = SWEEPS * CF
REST = (STENCIL - 1) * BS
ROW = 8
SPREAD = 2
AHEAD = 5
MESH = pl.DeviceIdType.MESH


def kernel(
    n_tm,
    n_space,
    columns,
    lists,
    coupling_hbm,
    retain_hbm,
    sources_hbm,
    guess_hbm,
    start_hbm,
    columns_hbm,
    values_out,
    residual_out,
    retain,
    sources,
    guess,
    start,
    coupling,
    own_weights,
    weights,
    forcing,
    guess_out,
    guess_in,
    retained,
    state,
    reached,
    doubled,
    parts,
    base,
    outbox,
    inbox,
    point_out,
    point_in,
    piece,
    far_coupling,
    far_weights,
    far_forcing_out,
    far_forcing,
    far_cells_out,
    far_cells,
    columns_own,
    far_slots_out,
    far_slots_in,
    far_slots,
    block_rows,
    block_forcing,
    block_cells,
    far_out,
    far_in,
    relay_in,
    far_parts,
    coupling_sem,
    input_sem,
    send_sem,
    recv_sem,
    slice_send,
    slice_recv,
    far_send,
    far_recv,
    spread_send,
    spread_recv,
    field_send,
    field_recv,
    relay_send,
    relay_recv,
):
    tm, space = lax.axis_index("tm"), lax.axis_index("space")
    before = [lax.rem(tm + n_tm - d, n_tm) for d in range(3)]
    after = [lax.rem(tm + d, n_tm) for d in range(3)]
    has = (space > 0, space < n_space - 1)
    beside = (space - 1, space + 1)
    place = lax.rem(space, ROW)
    across = ((place == 0) & has[0], (place == ROW - 1) & has[1])
    is_far = across[0] | across[1]
    is_relay = ((place == 1) & (space > 1)) | ((place == ROW - 2) & (space < n_space - 2))
    upper_half = (place >= ROW // 2).astype(jnp.int32)
    partner = space + 2 * upper_half - 1
    second = space + 4 * upper_half - 2
    rows_each = STENCIL * BS // n_tm

    lane = lax.broadcasted_iota(jnp.int32, (8, 128), 1)
    row = lax.broadcasted_iota(jnp.int32, (8, 128), 0)
    low, top = lane < BS, row < 4
    field = lax.rem(row, 4)

    loads = [
        pltpu.make_async_copy(
            coupling_hbm.at[pl.ds(BS * k, BS), :], coupling.at[pl.ds(BS * k, BS), :], coupling_sem.at[k]
        )
        for k in range(STENCIL)
    ]
    inputs = [
        pltpu.make_async_copy(source, target, input_sem.at[n])
        for n, (source, target) in enumerate(
            ((guess_hbm, guess), (sources_hbm, sources), (start_hbm, start), (retain_hbm, retain), (columns_hbm, columns_own))
        )
    ]
    for load in inputs + loads:
        load.start()

    def cells(p):
        return pl.ds(128 * p, 128)

    inbox[...] = jnp.zeros_like(inbox)
    barrier = pltpu.get_barrier_semaphore()
    for other in (before[1], before[2], after[1], after[2]):
        pl.semaphore_signal(barrier, inc=1, device_id={"tm": other}, device_id_type=MESH)
    for side in range(2):

        @pl.when(has[side])
        def _():
            pl.semaphore_signal(barrier, inc=1, device_id={"space": beside[side]}, device_id_type=MESH)

    @pl.when(is_far)
    def _():
        for d in range(3, n_tm - 2):
            pl.semaphore_signal(
                barrier, inc=1, device_id={"tm": lax.rem(tm + d, n_tm)}, device_id_type=MESH
            )

    @pl.when(is_far | is_relay)
    def _():
        pl.semaphore_signal(barrier, inc=1, device_id={"space": second}, device_id_type=MESH)

    for load in inputs[:2]:
        load.wait()
    for p in range(PAIRS):
        for f in range(C_DEV):
            guess_out[pl.ds(16 * f + p, 1), :] = guess[pl.ds(f, 1), cells(p)]
            forcing[pl.ds(64 * (4 + f) + 4 * p, 4), :] = sources[pl.ds(4 * f, 4), cells(p)]
    forcing[pl.ds(448, 64), :] = jnp.zeros((64, 128), jnp.float32)

    pl.semaphore_wait(
        barrier,
        4
        + has[0].astype(jnp.int32)
        + has[1].astype(jnp.int32)
        + (n_tm - 5) * is_far.astype(jnp.int32)
        + (is_far | is_relay).astype(jnp.int32),
    )

    def to_slice(n, source, target, other):
        return pltpu.make_async_remote_copy(
            src_ref=source,
            dst_ref=target,
            send_sem=slice_send.at[n],
            recv_sem=slice_recv.at[n],
            device_id={"tm": other},
            device_id_type=MESH,
        )

    def interval(a):
        return forcing.at[pl.ds(64 * a, 64), :]

    slice_copies = [
        to_slice(0, guess_out.at[pl.ds(16, 32), :], guess_in.at[pl.ds(0, 32), :], after[2]),
        to_slice(1, guess_out.at[pl.ds(0, 16), :], guess_in.at[pl.ds(32, 16), :], after[1]),
        to_slice(2, interval(6), interval(0), after[2]),
        to_slice(3, interval(4), interval(1), after[1]),
        to_slice(4, interval(5), interval(2), after[1]),
        to_slice(5, interval(6), interval(3), after[1]),
    ]
    for copy in slice_copies:
        copy.start()
    point_copy = to_slice(6, point_out, point_in, before[1])

    def halo_copy(slot, side):
        return pltpu.make_async_remote_copy(
            src_ref=outbox.at[slot, side],
            dst_ref=inbox.at[slot, 1 - side],
            send_sem=send_sem.at[slot, side],
            recv_sem=recv_sem.at[slot, 1 - side],
            device_id={"space": beside[side]},
            device_id_type=MESH,
        )

    def twice(value):
        turned = pltpu.roll(value, BS, 1)
        return jnp.where(low, value, turned), jnp.where(low, turned, value)

    def in_parts(value):
        upper = value.astype(jnp.bfloat16).astype(jnp.float32)
        return jnp.where(top, upper, value - upper)

    def to_partner(n, source, target):
        return pltpu.make_async_remote_copy(
            src_ref=source,
            dst_ref=target,
            send_sem=far_send.at[n],
            recv_sem=far_recv.at[n],
            device_id={"space": partner},
            device_id_type=MESH,
        )

    def rows_of(slice_at):
        return far_coupling.at[pl.ds(pl.multiple_of(rows_each * slice_at, 8), rows_each), :]

    far_copies = [
        to_partner(0, piece, rows_of(tm)),
        to_partner(1, far_forcing_out, far_forcing),
        to_partner(2, far_cells_out, far_cells),
        to_partner(3, far_slots_out, far_slots_in),
    ]

    def spread_copy(d, slice_at):
        return pltpu.make_async_remote_copy(
            src_ref=rows_of(slice_at),
            dst_ref=rows_of(slice_at),
            send_sem=spread_send.at[d],
            recv_sem=spread_recv.at[d],
            device_id={"tm": lax.rem(tm + d, n_tm)},
            device_id_type=MESH,
        )

    def field_copy(step):
        slot = lax.rem(step, 2)
        return pltpu.make_async_remote_copy(
            src_ref=far_out.at[slot],
            dst_ref=far_in.at[step],
            send_sem=field_send.at[slot],
            recv_sem=field_recv.at[step],
            device_id={"space": partner},
            device_id_type=MESH,
        )

    def relay_copy(step):
        slot = lax.rem(step, 2)
        return pltpu.make_async_remote_copy(
            src_ref=outbox.at[slot, upper_half],
            dst_ref=relay_in.at[step],
            send_sem=relay_send.at[slot],
            recv_sem=relay_recv.at[step],
            device_id={"space": second},
            device_id_type=MESH,
        )

    def near(step, side):
        return has[side] & jnp.logical_not(across[side] & (step >= AHEAD))

    def fields_go(step):
        return (step >= AHEAD - 1) & (step < STEPS - 1)

    def store_twice(target, p, rows, value):
        half = lax.broadcasted_iota(jnp.int32, value.shape, 1) < BS
        turned = pltpu.roll(value, BS, 1)
        target[2 * p, rows, :] = jnp.where(half, value, turned)
        target[2 * p + 1, rows, :] = jnp.where(half, turned, value)

    def of_listed(blocks, q):
        values = [blocks[lists[upper_half, 2 * q + h]] for h in range(2)]
        return jnp.where(lax.broadcasted_iota(jnp.int32, values[0].shape, 1) < BS, *values)

    def send(step, values):
        slot = lax.rem(step, 2)
        begins = jnp.where(lax.rem(step, CF) == 0, 4 - C_DEV * tm - step // CF, -1)
        for p in range(PAIRS):
            value = jnp.where(field == begins, start[pl.ds(p, 1), :], values[p])
            state[p] = value
            far_out[slot, pl.ds(4 * p, 4), :] = value[:4]
            doubled[2 * p], doubled[2 * p + 1] = twice(value)

        @pl.when(is_far & fields_go(step))
        def _():
            field_copy(step).start()

        for side in range(2):
            for q in range(HALO // 2):
                pair = jnp.where(low, doubled[lists[side, 2 * q]], doubled[lists[side, 2 * q + 1]])
                outbox[slot, side, pl.ds(4 * q, 4), :] = pair[:4]

            @pl.when(near(step, side))
            def _():
                halo_copy(slot, side).start()

        @pl.when(is_relay & fields_go(step))
        def _():
            relay_copy(step).start()

    for copy in slice_copies[:2]:
        copy.wait_recv()
    inputs[2].wait()
    first = []
    for p in range(PAIRS):
        rows = [guess_in[pl.ds(16 * f + p, 1), :] for f in range(C_DEV)]
        rows.append(jnp.zeros((1, 128), jnp.float32))
        first.append(jnp.concatenate(rows + rows, axis=0))
    send(jnp.int32(0), first)

    inputs[3].wait()
    inputs[4].wait()
    for p in range(PAIRS):
        retained[p] = jnp.where(top, retain[pl.ds(p, 1), :], 0.0)
    for load in loads:
        load.wait()

    @pl.when(is_far)
    def _():
        for p in range(PAIRS):
            own_rows = pl.ds(pl.multiple_of(rows_each * tm, 8), rows_each)
            store_twice(block_rows, p, pl.ds(0, rows_each), coupling[own_rows, cells(p)])
        for q in range(HALO // 2):
            piece[:, cells(q)] = of_listed(block_rows, q)
        far_copies[0].start()

    for k in range(STENCIL):
        target, at, gap = (own_weights, 0, BS) if k == 0 else (weights, BS * (k - 1), REST)

        @pl.loop(0, BS // 16)
        def _(n, k=k, target=target, at=at, gap=gap):
            entries = coupling[pl.ds(pl.multiple_of(BS * k + 16 * n, 16), 16), :]
            upper = entries.astype(jnp.bfloat16)
            target[pl.ds(pl.multiple_of(at + 16 * n, 16), 16), :] = upper
            target[pl.ds(pl.multiple_of(at + gap + 16 * n, 16), 16), :] = (
                entries - upper.astype(jnp.float32)
            ).astype(jnp.bfloat16)

    def on_diagonal(product):
        return [
            jnp.where(
                low,
                product[16 * h : 16 * h + 8, 128 * h : 128 * h + 128],
                product[16 * h + 8 : 16 * h + 16, 128 * h : 128 * h + 128],
            )
            for h in range(2)
        ]

    def four_rows(value):
        return twice(in_parts(jnp.concatenate([value, value], axis=0)))

    def listed_by_partner(step):
        slot = lax.rem(step, 2)
        field_copy(step).wait_recv()
        relay_copy(step).wait_recv()
        for p in range(PAIRS):
            far_parts[2 * p], far_parts[2 * p + 1] = four_rows(far_in[step, pl.ds(4 * p, 4), :])
        for q in range(HALO // 2):
            at = NBLK + HALO * upper_half + 2 * q
            far_parts[at], far_parts[at + 1] = four_rows(relay_in[step, pl.ds(4 * q, 4), :])
            at = NBLK + HALO * (1 - upper_half) + 2 * q
            far_parts[at], far_parts[at + 1] = four_rows(outbox[slot, upper_half, pl.ds(4 * q, 4), :])
        begins = jnp.where(lax.rem(step + 1, CF) == 0, 4 - C_DEV * tm - (step + 1) // CF, -1)
        for g in range(HALO // 4):
            picked, firsts = [], []
            for j in range(4 * g, 4 * g + 4):
                firsts.append(far_parts[far_slots[j, STENCIL - 1]])
                rest = [
                    jnp.where(
                        low,
                        far_parts[far_slots[j, k]],
                        far_parts[far_slots[j, k + 1]],
                    )
                    for k in range(0, STENCIL - 1, 2)
                ]
                picked.append(jnp.concatenate(rest + rest + firsts[-1:], axis=1))
            product = jnp.dot(
                jnp.concatenate(picked, axis=0).astype(jnp.bfloat16),
                far_weights[:, 256 * g : 256 * g + 256],
                preferred_element_type=jnp.float32,
            )
            for h, pair in enumerate(on_diagonal(product)):
                q = 2 * g + h
                heat = far_forcing[pl.ds(step + 32 * q, 4, stride=CF), :]
                heat = jnp.concatenate([heat, jnp.zeros((4, 128), jnp.float32)], axis=0)
                now = jnp.where(low, firsts[2 * h], firsts[2 * h + 1])
                total = pair + far_cells[pl.ds(q, 1), :] * now + heat
                value = total + pltpu.roll(total, 4, 0)
                value = jnp.where(field == begins, far_cells[pl.ds(8 + q, 1), :], value)
                inbox[1 - slot, upper_half, pl.ds(4 * q, 4), :] = value[:4]

    def one_step(step, carry):
        slot = lax.rem(step, 2)

        @pl.when(step == 0)
        def _():
            for copy in slice_copies[2:]:
                copy.wait_recv()

        @pl.when((step == 0) & is_far)
        def _():
            for p in range(PAIRS):
                for a in range(8):
                    store_twice(block_forcing, p, pl.ds(4 * a, 4), forcing[pl.ds(64 * a + 4 * p, 4), :])
                for n, source in enumerate((retain, start)):
                    store_twice(block_cells, p, pl.ds(n, 1), source[pl.ds(p, 1), :])
            for q in range(HALO // 2):
                far_forcing_out[pl.ds(32 * q, 32), :] = of_listed(block_forcing, q)
                both = of_listed(block_cells, q)
                far_cells_out[pl.ds(q, 1), :] = both[0:1]
                far_cells_out[pl.ds(8 + q, 1), :] = both[1:2]
            wide = lax.broadcasted_iota(jnp.int32, (HALO, NBLK), 0)
            listed = jnp.zeros((HALO, NBLK), jnp.int32)
            for j in range(HALO):
                listed = jnp.where(wide == j, lists[upper_half, j], listed)
            chosen = listed == lax.broadcasted_iota(jnp.int32, (HALO, NBLK), 1)
            place_at = lax.broadcasted_iota(jnp.int32, (HALO, 128), 1)
            table = jnp.zeros((HALO, 128), jnp.int32)
            for k in range(STENCIL):
                if k < STENCIL - 1:
                    found = jnp.where(chosen, columns_own[pl.ds(k, 1), :], 0)
                else:
                    found = jnp.where(chosen, listed, 0)
                table = jnp.where(place_at == k, jnp.sum(found, axis=1, keepdims=True), table)
            far_slots_out[...] = table
            for copy in far_copies[1:]:
                copy.start()

        @pl.when((step == SPREAD) & is_far)
        def _():
            far_copies[0].wait_recv()
            for d in range(1, n_tm):
                spread_copy(d, tm).start()

        @pl.when((step == AHEAD - 1) & is_far)
        def _():
            for copy in far_copies[1:]:
                copy.wait_recv()
            slots = pltpu.make_async_copy(far_slots_in, far_slots, input_sem.at[5])
            slots.start()
            slots.wait()
            for d in range(1, n_tm):
                spread_copy(d, lax.rem(tm + n_tm - d, n_tm)).wait_recv()
            for k in range(STENCIL):
                at, gap = (2 * REST, BS) if k == 0 else (BS * (k - 1), REST)

                @pl.loop(0, BS // 16)
                def _(n, k=k, at=at, gap=gap):
                    entries = far_coupling[pl.ds(pl.multiple_of(BS * k + 16 * n, 16), 16), :]
                    upper = entries.astype(jnp.bfloat16)
                    far_weights[pl.ds(pl.multiple_of(at + 16 * n, 16), 16), :] = upper
                    far_weights[pl.ds(pl.multiple_of(at + gap + 16 * n, 16), 16), :] = (
                        entries - upper.astype(jnp.float32)
                    ).astype(jnp.bfloat16)

        @pl.when(step == 4 * CF)
        def _():
            for p in range(PAIRS):
                value = reached[p]
                values_out[pl.ds(0, 2), cells(p)] = value[1:3]
                point_out[pl.ds(p, 1), :] = value[0:1]
            point_copy.start()

        at = (step // CF) * 64 + lax.rem(step, CF)
        for g in range(GROUPS):
            own = []
            for b in range(4 * g, 4 * g + 4):
                own.append(in_parts(doubled[b]))
                parts[b] = own[-1]
            product = jnp.dot(
                jnp.concatenate(own, axis=0).astype(jnp.bfloat16),
                own_weights[:, 256 * g : 256 * g + 256],
                preferred_element_type=jnp.float32,
            )
            for h, pair in enumerate(on_diagonal(product)):
                p = 2 * g + h
                heat = forcing[pl.ds(at + 4 * p, 4, stride=64), :]
                heat = jnp.concatenate([heat, jnp.zeros((4, 128), jnp.float32)], axis=0)
                base[p] = pair + retained[p] * state[p] + heat

        @pl.when(is_far & (step >= AHEAD))
        def _():
            listed_by_partner(step - 1)

        for side in range(2):

            @pl.when(near(step, side))
            def _():
                halo_copy(slot, 1 - side).wait_recv()

        for side in range(2):
            for q in range(HALO // 2):
                value = inbox[slot, side, pl.ds(4 * q, 4), :]
                n = NBLK + HALO * side + 2 * q
                parts[n], parts[n + 1] = four_rows(value)

        values = []
        for g in range(GROUPS):
            picked = []
            for b in range(4 * g, 4 * g + 4):
                picked.append(
                    jnp.concatenate(
                        [
                            jnp.where(low, parts[columns[k, b]], parts[columns[k + 1, b]])
                            for k in range(0, STENCIL - 1, 2)
                        ],
                        axis=1,
                    )
                )
            left = jnp.concatenate(picked, axis=0).astype(jnp.bfloat16)
            product = jnp.dot(
                jnp.concatenate([left, left], axis=1),
                weights[:, 256 * g : 256 * g + 256],
                preferred_element_type=jnp.float32,
            )
            for h, pair in enumerate(on_diagonal(product)):
                total = base[2 * g + h] + pair
                values.append(total + pltpu.roll(total, 4, 0))
                reached[2 * g + h] = values[-1]

        for side in range(2):

            @pl.when(near(step, side))
            def _():
                halo_copy(slot, side).wait_send()

        @pl.when(is_far & fields_go(step))
        def _():
            field_copy(step).wait_send()

        @pl.when(is_relay & fields_go(step))
        def _():
            relay_copy(step).wait_send()

        @pl.when(step < STEPS - 1)
        def _():
            send(step + 1, [reached[p] for p in range(PAIRS)])

        return carry

    lax.fori_loop(0, STEPS, one_step, 0)

    for copy in slice_copies:
        copy.wait_send()

    @pl.when(is_far)
    def _():
        for copy in far_copies:
            copy.wait_send()
        for d in range(1, n_tm):
            spread_copy(d, tm).wait_send()

    point_copy.wait()
    for p in range(PAIRS):
        values_out[pl.ds(2, 1), cells(p)] = point_in[pl.ds(p, 1), :]
        residual_out[:, cells(p)] = reached[p][:3] - values_out[:, cells(p)]


def body(n_tm, n_space, coupling, retain, sources, initial_guess, start_field, block_columns, send_lists):
    count = retain.shape[0]
    f32, bf16 = jnp.float32, jnp.bfloat16
    smem, vmem = (pl.BlockSpec(memory_space=space) for space in (pltpu.SMEM, pltpu.VMEM))
    return pl.pallas_call(
        functools.partial(kernel, n_tm, n_space),
        out_shape=(jax.ShapeDtypeStruct((C_DEV, count), f32),) * 2,
        in_specs=[smem, smem] + [pl.BlockSpec(memory_space=pl.ANY)] * 6,
        out_specs=(vmem, vmem),
        scratch_shapes=[
            pltpu.VMEM((PAIRS, 128), f32),
            pltpu.VMEM((C_DEV * CF, count), f32),
            pltpu.VMEM((C_DEV, count), f32),
            pltpu.VMEM((PAIRS, 128), f32),
            pltpu.VMEM((STENCIL * BS, count), f32),
            pltpu.VMEM((2 * BS, count), bf16),
            pltpu.VMEM((2 * REST, count), bf16),
            pltpu.VMEM((512, 128), f32),
            pltpu.VMEM((48, 128), f32),
            pltpu.VMEM((48, 128), f32),
            pltpu.VMEM((PAIRS, 8, 128), f32),
            pltpu.VMEM((PAIRS, 8, 128), f32),
            pltpu.VMEM((PAIRS, 8, 128), f32),
            pltpu.VMEM((NBLK, 8, 128), f32),
            pltpu.VMEM((NBLK + 2 * HALO, 8, 128), f32),
            pltpu.VMEM((PAIRS, 8, 128), f32),
            pltpu.VMEM((2, 2, 32, 128), f32),
            pltpu.VMEM((2, 2, 32, 128), f32),
            pltpu.VMEM((16, 128), f32),
            pltpu.VMEM((16, 128), f32),
            pltpu.VMEM((STENCIL * BS // n_tm, count // 2), f32),
            pltpu.VMEM((STENCIL * BS, count // 2), f32),
            pltpu.VMEM((2 * STENCIL * BS, count // 2), bf16),
            pltpu.VMEM((256, 128), f32),
            pltpu.VMEM((256, 128), f32),
            pltpu.VMEM((16, 128), f32),
            pltpu.VMEM((16, 128), f32),
            pltpu.VMEM((STENCIL - 1, NBLK), jnp.int32),
            pltpu.VMEM((HALO, 128), jnp.int32),
            pltpu.VMEM((HALO, 128), jnp.int32),
            pltpu.SMEM((HALO, 128), jnp.int32),
            pltpu.VMEM((NBLK, STENCIL * BS // n_tm, 128), f32),
            pltpu.VMEM((NBLK, 32, 128), f32),
            pltpu.VMEM((NBLK, 8, 128), f32),
            pltpu.VMEM((2, 64, 128), f32),
            pltpu.VMEM((STEPS, 64, 128), f32),
            pltpu.VMEM((STEPS, 32, 128), f32),
            pltpu.VMEM((NBLK + 2 * HALO, 8, 128), f32),
            pltpu.SemaphoreType.DMA((STENCIL,)),
            pltpu.SemaphoreType.DMA((6,)),
            pltpu.SemaphoreType.DMA((2, 2)),
            pltpu.SemaphoreType.DMA((2, 2)),
            pltpu.SemaphoreType.DMA((7,)),
            pltpu.SemaphoreType.DMA((7,)),
            pltpu.SemaphoreType.DMA((4,)),
            pltpu.SemaphoreType.DMA((4,)),
            pltpu.SemaphoreType.DMA((n_tm,)),
            pltpu.SemaphoreType.DMA((n_tm,)),
            pltpu.SemaphoreType.DMA((2,)),
            pltpu.SemaphoreType.DMA((STEPS,)),
            pltpu.SemaphoreType.DMA((2,)),
            pltpu.SemaphoreType.DMA((STEPS,)),
        ],
        compiler_params=pltpu.CompilerParams(
            collective_id=0, has_side_effects=True, vmem_limit_bytes=60 * 2**20
        ),
    )(
        block_columns.T,
        send_lists,
        coupling,
        retain.reshape(PAIRS, 128),
        sources,
        initial_guess,
        start_field.reshape(PAIRS, 128),
        block_columns.T,
    )


def solution(mesh):
    placed = (
        P(None, "space"),
        P("space"),
        P("tm", "space"),
        P("tm", "space"),
        P("space"),
        P("space", None),
        P("space", None),
    )
    return jax.shard_map(
        functools.partial(body, mesh.shape["tm"], mesh.shape["space"]),
        mesh=mesh,
        in_specs=placed,
        out_specs=(P("tm", "space"), P("tm", "space")),
        check_vma=False,
    )
```

```python
import functools

import jax
import jax.numpy as jnp
from jax import lax
from jax.experimental import pallas as pl
from jax.experimental.pallas import tpu as pltpu
from jax.sharding import PartitionSpec as P

BS = 64
STENCIL = 7
NBLK = 32
CF = 4
C_DEV = 3
SWEEPS = 5
HALO = 16
PAIRS = NBLK // 2
GROUPS = NBLK // 4
STEPS = SWEEPS * CF
REST = (STENCIL - 1) * BS
ROW = 8
SPREAD = 1
AHEAD = 4
MESH = pl.DeviceIdType.MESH


def kernel(
    n_tm,
    n_space,
    columns,
    lists,
    coupling_hbm,
    retain_hbm,
    sources_hbm,
    guess_hbm,
    start_hbm,
    columns_hbm,
    values_out,
    residual_out,
    retain,
    sources,
    guess,
    start,
    coupling,
    own_weights,
    weights,
    forcing,
    guess_out,
    guess_in,
    retained,
    state,
    reached,
    doubled,
    parts,
    base,
    outbox,
    inbox,
    point_out,
    point_in,
    piece,
    far_coupling,
    far_weights,
    far_forcing_out,
    far_forcing,
    far_cells_out,
    far_cells,
    columns_own,
    far_slots_out,
    far_slots_in,
    far_slots,
    block_rows,
    block_forcing,
    block_cells,
    far_out,
    far_in,
    relay_in,
    far_parts,
    coupling_sem,
    input_sem,
    send_sem,
    recv_sem,
    slice_send,
    slice_recv,
    far_send,
    far_recv,
    spread_send,
    spread_recv,
    field_send,
    field_recv,
    relay_send,
    relay_recv,
):
    tm, space = lax.axis_index("tm"), lax.axis_index("space")
    before = [lax.rem(tm + n_tm - d, n_tm) for d in range(3)]
    after = [lax.rem(tm + d, n_tm) for d in range(3)]
    has = (space > 0, space < n_space - 1)
    beside = (space - 1, space + 1)
    place = lax.rem(space, ROW)
    across = ((place == 0) & has[0], (place == ROW - 1) & has[1])
    is_far = across[0] | across[1]
    is_relay = ((place == 1) & (space > 1)) | ((place == ROW - 2) & (space < n_space - 2))
    upper_half = (place >= ROW // 2).astype(jnp.int32)
    partner = space + 2 * upper_half - 1
    second = space + 4 * upper_half - 2
    rows_each = STENCIL * BS // n_tm

    lane = lax.broadcasted_iota(jnp.int32, (8, 128), 1)
    row = lax.broadcasted_iota(jnp.int32, (8, 128), 0)
    low, top = lane < BS, row < 4
    field = lax.rem(row, 4)

    loads = [
        pltpu.make_async_copy(
            coupling_hbm.at[pl.ds(BS * k, BS), :], coupling.at[pl.ds(BS * k, BS), :], coupling_sem.at[k]
        )
        for k in range(STENCIL)
    ]
    inputs = [
        pltpu.make_async_copy(source, target, input_sem.at[n])
        for n, (source, target) in enumerate(
            ((guess_hbm, guess), (sources_hbm, sources), (start_hbm, start), (retain_hbm, retain), (columns_hbm, columns_own))
        )
    ]
    for load in inputs + loads:
        load.start()

    def cells(p):
        return pl.ds(128 * p, 128)

    inbox[...] = jnp.zeros_like(inbox)
    barrier = pltpu.get_barrier_semaphore()
    for other in (before[1], before[2], after[1], after[2]):
        pl.semaphore_signal(barrier, inc=1, device_id={"tm": other}, device_id_type=MESH)
    for side in range(2):

        @pl.when(has[side])
        def _():
            pl.semaphore_signal(barrier, inc=1, device_id={"space": beside[side]}, device_id_type=MESH)

    @pl.when(is_far)
    def _():
        for d in range(3, n_tm - 2):
            pl.semaphore_signal(
                barrier, inc=1, device_id={"tm": lax.rem(tm + d, n_tm)}, device_id_type=MESH
            )

    @pl.when(is_far | is_relay)
    def _():
        pl.semaphore_signal(barrier, inc=1, device_id={"space": second}, device_id_type=MESH)

    for load in inputs[:2]:
        load.wait()
    for p in range(PAIRS):
        for f in range(C_DEV):
            guess_out[pl.ds(16 * f + p, 1), :] = guess[pl.ds(f, 1), cells(p)]
            forcing[pl.ds(64 * (4 + f) + 4 * p, 4), :] = sources[pl.ds(4 * f, 4), cells(p)]
    forcing[pl.ds(448, 64), :] = jnp.zeros((64, 128), jnp.float32)

    def to_slice(n, source, target, other):
        return pltpu.make_async_remote_copy(
            src_ref=source,
            dst_ref=target,
            send_sem=slice_send.at[n],
            recv_sem=slice_recv.at[n],
            device_id={"tm": other},
            device_id_type=MESH,
        )

    def interval(a):
        return forcing.at[pl.ds(64 * a, 64), :]

    slice_copies = [
        to_slice(0, guess_out.at[pl.ds(16, 32), :], guess_in.at[pl.ds(0, 32), :], after[2]),
        to_slice(1, guess_out.at[pl.ds(0, 16), :], guess_in.at[pl.ds(32, 16), :], after[1]),
        to_slice(2, interval(6), interval(0), after[2]),
        to_slice(3, interval(4), interval(1), after[1]),
        to_slice(4, interval(5), interval(2), after[1]),
        to_slice(5, interval(6), interval(3), after[1]),
    ]
    point_copy = to_slice(6, point_out, point_in, before[1])

    def halo_copy(slot, side):
        return pltpu.make_async_remote_copy(
            src_ref=outbox.at[slot, side],
            dst_ref=inbox.at[slot, 1 - side],
            send_sem=send_sem.at[slot, side],
            recv_sem=recv_sem.at[slot, 1 - side],
            device_id={"space": beside[side]},
            device_id_type=MESH,
        )

    def twice(value):
        turned = pltpu.roll(value, BS, 1)
        return jnp.where(low, value, turned), jnp.where(low, turned, value)

    def in_parts(value):
        upper = value.astype(jnp.bfloat16).astype(jnp.float32)
        return jnp.where(top, upper, value - upper)

    def to_partner(n, source, target):
        return pltpu.make_async_remote_copy(
            src_ref=source,
            dst_ref=target,
            send_sem=far_send.at[n],
            recv_sem=far_recv.at[n],
            device_id={"space": partner},
            device_id_type=MESH,
        )

    def rows_of(slice_at):
        return far_coupling.at[pl.ds(pl.multiple_of(rows_each * slice_at, 8), rows_each), :]

    far_copies = [
        to_partner(0, piece, rows_of(tm)),
        to_partner(1, far_forcing_out, far_forcing),
        to_partner(2, far_cells_out, far_cells),
        to_partner(3, far_slots_out, far_slots_in),
    ]

    def spread_copy(d, slice_at):
        return pltpu.make_async_remote_copy(
            src_ref=rows_of(slice_at),
            dst_ref=rows_of(slice_at),
            send_sem=spread_send.at[d],
            recv_sem=spread_recv.at[d],
            device_id={"tm": lax.rem(tm + d, n_tm)},
            device_id_type=MESH,
        )

    def field_copy(step):
        slot = lax.rem(step, 2)
        return pltpu.make_async_remote_copy(
            src_ref=far_out.at[slot],
            dst_ref=far_in.at[step],
            send_sem=field_send.at[slot],
            recv_sem=field_recv.at[step],
            device_id={"space": partner},
            device_id_type=MESH,
        )

    def relay_copy(step):
        slot = lax.rem(step, 2)
        return pltpu.make_async_remote_copy(
            src_ref=outbox.at[slot, upper_half],
            dst_ref=relay_in.at[step],
            send_sem=relay_send.at[slot],
            recv_sem=relay_recv.at[step],
            device_id={"space": second},
            device_id_type=MESH,
        )

    def near(step, side):
        return has[side] & jnp.logical_not(across[side] & (step >= AHEAD))

    def fields_go(step):
        return (step >= AHEAD - 1) & (step < STEPS - 1)

    def store_twice(target, p, rows, value):
        half = lax.broadcasted_iota(jnp.int32, value.shape, 1) < BS
        turned = pltpu.roll(value, BS, 1)
        target[2 * p, rows, :] = jnp.where(half, value, turned)
        target[2 * p + 1, rows, :] = jnp.where(half, turned, value)

    def of_listed(blocks, q):
        values = [blocks[lists[upper_half, 2 * q + h]] for h in range(2)]
        return jnp.where(lax.broadcasted_iota(jnp.int32, values[0].shape, 1) < BS, *values)

    def send(step, values):
        slot = lax.rem(step, 2)
        begins = jnp.where(lax.rem(step, CF) == 0, 4 - C_DEV * tm - step // CF, -1)
        for p in range(PAIRS):
            value = jnp.where(field == begins, start[pl.ds(p, 1), :], values[p])
            state[p] = value
            far_out[slot, pl.ds(4 * p, 4), :] = value[:4]
            doubled[2 * p], doubled[2 * p + 1] = twice(value)

        @pl.when(is_far & fields_go(step))
        def _():
            field_copy(step).start()

        for side in range(2):
            for q in range(HALO // 2):
                pair = jnp.where(low, doubled[lists[side, 2 * q]], doubled[lists[side, 2 * q + 1]])
                outbox[slot, side, pl.ds(4 * q, 4), :] = pair[:4]

            @pl.when(near(step, side))
            def _():
                halo_copy(slot, side).start()

        @pl.when(is_relay & fields_go(step))
        def _():
            relay_copy(step).start()

    @pl.when(is_far)
    def _():
        for load in loads:
            load.wait()
        for p in range(PAIRS):
            own_rows = pl.ds(pl.multiple_of(rows_each * tm, 8), rows_each)
            store_twice(block_rows, p, pl.ds(0, rows_each), coupling[own_rows, cells(p)])
        for q in range(HALO // 2):
            piece[:, cells(q)] = of_listed(block_rows, q)

    pl.semaphore_wait(
        barrier,
        4
        + has[0].astype(jnp.int32)
        + has[1].astype(jnp.int32)
        + (n_tm - 5) * is_far.astype(jnp.int32)
        + (is_far | is_relay).astype(jnp.int32),
    )


    for copy in slice_copies[:2]:
        copy.start()

    @pl.when(is_far)
    def _():
        far_copies[0].start()

    for copy in slice_copies[2:]:
        copy.start()
    for copy in slice_copies[:2]:
        copy.wait_recv()
    inputs[2].wait()
    first = []
    for p in range(PAIRS):
        rows = [guess_in[pl.ds(16 * f + p, 1), :] for f in range(C_DEV)]
        rows.append(jnp.zeros((1, 128), jnp.float32))
        first.append(jnp.concatenate(rows + rows, axis=0))
    send(jnp.int32(0), first)

    inputs[3].wait()
    inputs[4].wait()
    for p in range(PAIRS):
        retained[p] = jnp.where(top, retain[pl.ds(p, 1), :], 0.0)
    @pl.when(jnp.logical_not(is_far))
    def _():
        for load in loads:
            load.wait()

    for k in range(STENCIL):
        target, at, gap = (own_weights, 0, BS) if k == 0 else (weights, BS * (k - 1), REST)

        @pl.loop(0, BS // 16)
        def _(n, k=k, target=target, at=at, gap=gap):
            entries = coupling[pl.ds(pl.multiple_of(BS * k + 16 * n, 16), 16), :]
            upper = entries.astype(jnp.bfloat16)
            target[pl.ds(pl.multiple_of(at + 16 * n, 16), 16), :] = upper
            target[pl.ds(pl.multiple_of(at + gap + 16 * n, 16), 16), :] = (
                entries - upper.astype(jnp.float32)
            ).astype(jnp.bfloat16)

    def on_diagonal(product):
        return [
            jnp.where(
                low,
                product[16 * h : 16 * h + 8, 128 * h : 128 * h + 128],
                product[16 * h + 8 : 16 * h + 16, 128 * h : 128 * h + 128],
            )
            for h in range(2)
        ]

    def four_rows(value):
        return twice(in_parts(jnp.concatenate([value, value], axis=0)))

    def listed_by_partner(step):
        slot = lax.rem(step, 2)
        field_copy(step).wait_recv()
        relay_copy(step).wait_recv()
        for p in range(PAIRS):
            far_parts[2 * p], far_parts[2 * p + 1] = four_rows(far_in[step, pl.ds(4 * p, 4), :])
        for q in range(HALO // 2):
            at = NBLK + HALO * upper_half + 2 * q
            far_parts[at], far_parts[at + 1] = four_rows(relay_in[step, pl.ds(4 * q, 4), :])
            at = NBLK + HALO * (1 - upper_half) + 2 * q
            far_parts[at], far_parts[at + 1] = four_rows(outbox[slot, upper_half, pl.ds(4 * q, 4), :])
        begins = jnp.where(lax.rem(step + 1, CF) == 0, 4 - C_DEV * tm - (step + 1) // CF, -1)
        for g in range(HALO // 4):
            picked, firsts = [], []
            for j in range(4 * g, 4 * g + 4):
                firsts.append(far_parts[far_slots[j, STENCIL - 1]])
                rest = [
                    jnp.where(
                        low,
                        far_parts[far_slots[j, k]],
                        far_parts[far_slots[j, k + 1]],
                    )
                    for k in range(0, STENCIL - 1, 2)
                ]
                picked.append(jnp.concatenate(rest + rest + firsts[-1:], axis=1))
            product = jnp.dot(
                jnp.concatenate(picked, axis=0).astype(jnp.bfloat16),
                far_weights[:, 256 * g : 256 * g + 256],
                preferred_element_type=jnp.float32,
            )
            for h, pair in enumerate(on_diagonal(product)):
                q = 2 * g + h
                heat = far_forcing[pl.ds(step + 32 * q, 4, stride=CF), :]
                heat = jnp.concatenate([heat, jnp.zeros((4, 128), jnp.float32)], axis=0)
                now = jnp.where(low, firsts[2 * h], firsts[2 * h + 1])
                total = pair + far_cells[pl.ds(q, 1), :] * now + heat
                value = total + pltpu.roll(total, 4, 0)
                value = jnp.where(field == begins, far_cells[pl.ds(8 + q, 1), :], value)
                inbox[1 - slot, upper_half, pl.ds(4 * q, 4), :] = value[:4]

    def one_step(step, carry):
        slot = lax.rem(step, 2)

        @pl.when(step == 0)
        def _():
            for copy in slice_copies[2:]:
                copy.wait_recv()

        @pl.when((step == 0) & is_far)
        def _():
            for p in range(PAIRS):
                for a in range(8):
                    store_twice(block_forcing, p, pl.ds(4 * a, 4), forcing[pl.ds(64 * a + 4 * p, 4), :])
                for n, source in enumerate((retain, start)):
                    store_twice(block_cells, p, pl.ds(n, 1), source[pl.ds(p, 1), :])
            for q in range(HALO // 2):
                far_forcing_out[pl.ds(32 * q, 32), :] = of_listed(block_forcing, q)
                both = of_listed(block_cells, q)
                far_cells_out[pl.ds(q, 1), :] = both[0:1]
                far_cells_out[pl.ds(8 + q, 1), :] = both[1:2]
            wide = lax.broadcasted_iota(jnp.int32, (HALO, NBLK), 0)
            listed = jnp.zeros((HALO, NBLK), jnp.int32)
            for j in range(HALO):
                listed = jnp.where(wide == j, lists[upper_half, j], listed)
            chosen = listed == lax.broadcasted_iota(jnp.int32, (HALO, NBLK), 1)
            place_at = lax.broadcasted_iota(jnp.int32, (HALO, 128), 1)
            table = jnp.zeros((HALO, 128), jnp.int32)
            for k in range(STENCIL):
                if k < STENCIL - 1:
                    found = jnp.where(chosen, columns_own[pl.ds(k, 1), :], 0)
                else:
                    found = jnp.where(chosen, listed, 0)
                table = jnp.where(place_at == k, jnp.sum(found, axis=1, keepdims=True), table)
            far_slots_out[...] = table
            for copy in far_copies[1:]:
                copy.start()

        @pl.when((step == SPREAD) & is_far)
        def _():
            far_copies[0].wait_recv()
            for d in range(1, n_tm):
                spread_copy(d, tm).start()

        @pl.when((step == AHEAD - 1) & is_far)
        def _():
            for copy in far_copies[1:]:
                copy.wait_recv()
            slots = pltpu.make_async_copy(far_slots_in, far_slots, input_sem.at[5])
            slots.start()
            slots.wait()
            for d in range(1, n_tm):
                spread_copy(d, lax.rem(tm + n_tm - d, n_tm)).wait_recv()
            for k in range(STENCIL):
                at, gap = (2 * REST, BS) if k == 0 else (BS * (k - 1), REST)

                @pl.loop(0, BS // 16)
                def _(n, k=k, at=at, gap=gap):
                    entries = far_coupling[pl.ds(pl.multiple_of(BS * k + 16 * n, 16), 16), :]
                    upper = entries.astype(jnp.bfloat16)
                    far_weights[pl.ds(pl.multiple_of(at + 16 * n, 16), 16), :] = upper
                    far_weights[pl.ds(pl.multiple_of(at + gap + 16 * n, 16), 16), :] = (
                        entries - upper.astype(jnp.float32)
                    ).astype(jnp.bfloat16)

        @pl.when(step == 4 * CF)
        def _():
            for p in range(PAIRS):
                value = reached[p]
                values_out[pl.ds(0, 2), cells(p)] = value[1:3]
                point_out[pl.ds(p, 1), :] = value[0:1]
            point_copy.start()

        at = (step // CF) * 64 + lax.rem(step, CF)
        for g in range(GROUPS):
            own = []
            for b in range(4 * g, 4 * g + 4):
                own.append(in_parts(doubled[b]))
                parts[b] = own[-1]
            product = jnp.dot(
                jnp.concatenate(own, axis=0).astype(jnp.bfloat16),
                own_weights[:, 256 * g : 256 * g + 256],
                preferred_element_type=jnp.float32,
            )
            for h, pair in enumerate(on_diagonal(product)):
                p = 2 * g + h
                heat = forcing[pl.ds(at + 4 * p, 4, stride=64), :]
                heat = jnp.concatenate([heat, jnp.zeros((4, 128), jnp.float32)], axis=0)
                base[p] = pair + retained[p] * state[p] + heat

        @pl.when(is_far & (step >= AHEAD))
        def _():
            listed_by_partner(step - 1)

        for side in range(2):

            @pl.when(near(step, side))
            def _():
                halo_copy(slot, 1 - side).wait_recv()

        for side in range(2):
            for q in range(HALO // 2):
                value = inbox[slot, side, pl.ds(4 * q, 4), :]
                n = NBLK + HALO * side + 2 * q
                parts[n], parts[n + 1] = four_rows(value)

        values = []
        for g in range(GROUPS):
            picked = []
            for b in range(4 * g, 4 * g + 4):
                picked.append(
                    jnp.concatenate(
                        [
                            jnp.where(low, parts[columns[k, b]], parts[columns[k + 1, b]])
                            for k in range(0, STENCIL - 1, 2)
                        ],
                        axis=1,
                    )
                )
            left = jnp.concatenate(picked, axis=0).astype(jnp.bfloat16)
            product = jnp.dot(
                jnp.concatenate([left, left], axis=1),
                weights[:, 256 * g : 256 * g + 256],
                preferred_element_type=jnp.float32,
            )
            for h, pair in enumerate(on_diagonal(product)):
                total = base[2 * g + h] + pair
                values.append(total + pltpu.roll(total, 4, 0))
                reached[2 * g + h] = values[-1]

        for side in range(2):

            @pl.when(near(step, side))
            def _():
                halo_copy(slot, side).wait_send()

        @pl.when(is_far & fields_go(step))
        def _():
            field_copy(step).wait_send()

        @pl.when(is_relay & fields_go(step))
        def _():
            relay_copy(step).wait_send()

        @pl.when(step < STEPS - 1)
        def _():
            send(step + 1, [reached[p] for p in range(PAIRS)])

        return carry

    lax.fori_loop(0, STEPS, one_step, 0)

    for copy in slice_copies:
        copy.wait_send()

    @pl.when(is_far)
    def _():
        for copy in far_copies:
            copy.wait_send()
        for d in range(1, n_tm):
            spread_copy(d, tm).wait_send()

    point_copy.wait()
    for p in range(PAIRS):
        values_out[pl.ds(2, 1), cells(p)] = point_in[pl.ds(p, 1), :]
        residual_out[:, cells(p)] = reached[p][:3] - values_out[:, cells(p)]


def body(n_tm, n_space, coupling, retain, sources, initial_guess, start_field, block_columns, send_lists):
    count = retain.shape[0]
    f32, bf16 = jnp.float32, jnp.bfloat16
    smem, vmem = (pl.BlockSpec(memory_space=space) for space in (pltpu.SMEM, pltpu.VMEM))
    return pl.pallas_call(
        functools.partial(kernel, n_tm, n_space),
        out_shape=(jax.ShapeDtypeStruct((C_DEV, count), f32),) * 2,
        in_specs=[smem, smem] + [pl.BlockSpec(memory_space=pl.ANY)] * 6,
        out_specs=(vmem, vmem),
        scratch_shapes=[
            pltpu.VMEM((PAIRS, 128), f32),
            pltpu.VMEM((C_DEV * CF, count), f32),
            pltpu.VMEM((C_DEV, count), f32),
            pltpu.VMEM((PAIRS, 128), f32),
            pltpu.VMEM((STENCIL * BS, count), f32),
            pltpu.VMEM((2 * BS, count), bf16),
            pltpu.VMEM((2 * REST, count), bf16),
            pltpu.VMEM((512, 128), f32),
            pltpu.VMEM((48, 128), f32),
            pltpu.VMEM((48, 128), f32),
            pltpu.VMEM((PAIRS, 8, 128), f32),
            pltpu.VMEM((PAIRS, 8, 128), f32),
            pltpu.VMEM((PAIRS, 8, 128), f32),
            pltpu.VMEM((NBLK, 8, 128), f32),
            pltpu.VMEM((NBLK + 2 * HALO, 8, 128), f32),
            pltpu.VMEM((PAIRS, 8, 128), f32),
            pltpu.VMEM((2, 2, 32, 128), f32),
            pltpu.VMEM((2, 2, 32, 128), f32),
            pltpu.VMEM((16, 128), f32),
            pltpu.VMEM((16, 128), f32),
            pltpu.VMEM((STENCIL * BS // n_tm, count // 2), f32),
            pltpu.VMEM((STENCIL * BS, count // 2), f32),
            pltpu.VMEM((2 * STENCIL * BS, count // 2), bf16),
            pltpu.VMEM((256, 128), f32),
            pltpu.VMEM((256, 128), f32),
            pltpu.VMEM((16, 128), f32),
            pltpu.VMEM((16, 128), f32),
            pltpu.VMEM((STENCIL - 1, NBLK), jnp.int32),
            pltpu.VMEM((HALO, 128), jnp.int32),
            pltpu.VMEM((HALO, 128), jnp.int32),
            pltpu.SMEM((HALO, 128), jnp.int32),
            pltpu.VMEM((NBLK, STENCIL * BS // n_tm, 128), f32),
            pltpu.VMEM((NBLK, 32, 128), f32),
            pltpu.VMEM((NBLK, 8, 128), f32),
            pltpu.VMEM((2, 64, 128), f32),
            pltpu.VMEM((STEPS, 64, 128), f32),
            pltpu.VMEM((STEPS, 32, 128), f32),
            pltpu.VMEM((NBLK + 2 * HALO, 8, 128), f32),
            pltpu.SemaphoreType.DMA((STENCIL,)),
            pltpu.SemaphoreType.DMA((6,)),
            pltpu.SemaphoreType.DMA((2, 2)),
            pltpu.SemaphoreType.DMA((2, 2)),
            pltpu.SemaphoreType.DMA((7,)),
            pltpu.SemaphoreType.DMA((7,)),
            pltpu.SemaphoreType.DMA((4,)),
            pltpu.SemaphoreType.DMA((4,)),
            pltpu.SemaphoreType.DMA((n_tm,)),
            pltpu.SemaphoreType.DMA((n_tm,)),
            pltpu.SemaphoreType.DMA((2,)),
            pltpu.SemaphoreType.DMA((STEPS,)),
            pltpu.SemaphoreType.DMA((2,)),
            pltpu.SemaphoreType.DMA((STEPS,)),
        ],
        compiler_params=pltpu.CompilerParams(
            collective_id=0, has_side_effects=True, vmem_limit_bytes=60 * 2**20
        ),
    )(
        block_columns.T,
        send_lists,
        coupling,
        retain.reshape(PAIRS, 128),
        sources,
        initial_guess,
        start_field.reshape(PAIRS, 128),
        block_columns.T,
    )


def solution(mesh):
    placed = (
        P(None, "space"),
        P("space"),
        P("tm", "space"),
        P("tm", "space"),
        P("space"),
        P("space", None),
        P("space", None),
    )
    return jax.shard_map(
        functools.partial(body, mesh.shape["tm"], mesh.shape["space"]),
        mesh=mesh,
        in_specs=placed,
        out_specs=(P("tm", "space"), P("tm", "space")),
        check_vma=False,
    )
```

```python
import functools

import jax
import jax.numpy as jnp
from jax import lax
from jax.experimental import pallas as pl
from jax.experimental.pallas import tpu as pltpu
from jax.sharding import PartitionSpec as P

BS = 64
STENCIL = 7
NBLK = 32
CF = 4
C_DEV = 3
SWEEPS = 5
HALO = 16
PAIRS = NBLK // 2
GROUPS = NBLK // 4
STEPS = SWEEPS * CF
REST = (STENCIL - 1) * BS
ROW = 8
SPREAD = 1
AHEAD = 4
MESH = pl.DeviceIdType.MESH


def kernel(
    n_tm,
    n_space,
    lists_hbm,
    coupling_hbm,
    retain_hbm,
    sources_hbm,
    guess_hbm,
    start_hbm,
    columns_hbm,
    values_out,
    residual_out,
    columns,
    lists,
    retain,
    sources,
    guess,
    start,
    coupling,
    own_weights,
    weights,
    forcing,
    guess_out,
    guess_in,
    retained,
    state,
    reached,
    doubled,
    parts,
    base,
    outbox,
    inbox,
    point_out,
    point_in,
    piece,
    far_coupling,
    far_weights,
    far_forcing_out,
    far_forcing,
    far_cells_out,
    far_cells,
    columns_own,
    far_slots_out,
    far_slots_in,
    far_slots,
    block_rows,
    block_forcing,
    block_cells,
    far_out,
    far_in,
    relay_in,
    far_parts,
    coupling_sem,
    input_sem,
    send_sem,
    recv_sem,
    slice_send,
    slice_recv,
    far_send,
    far_recv,
    spread_send,
    spread_recv,
    field_send,
    field_recv,
    relay_send,
    relay_recv,
):
    tm, space = lax.axis_index("tm"), lax.axis_index("space")
    before = [lax.rem(tm + n_tm - d, n_tm) for d in range(3)]
    after = [lax.rem(tm + d, n_tm) for d in range(3)]
    has = (space > 0, space < n_space - 1)
    beside = (space - 1, space + 1)
    place = lax.rem(space, ROW)
    across = ((place == 0) & has[0], (place == ROW - 1) & has[1])
    is_far = across[0] | across[1]
    is_relay = ((place == 1) & (space > 1)) | ((place == ROW - 2) & (space < n_space - 2))
    upper_half = (place >= ROW // 2).astype(jnp.int32)
    partner = space + 2 * upper_half - 1
    second = space + 4 * upper_half - 2
    rows_each = STENCIL * BS // n_tm
    cross = lax.rem(space, 2)

    lane = lax.broadcasted_iota(jnp.int32, (8, 128), 1)
    row = lax.broadcasted_iota(jnp.int32, (8, 128), 0)
    low, top = lane < BS, row < 4
    field = lax.rem(row, 4)

    loads = [
        pltpu.make_async_copy(
            coupling_hbm.at[pl.ds(BS * k, BS), :], coupling.at[pl.ds(BS * k, BS), :], coupling_sem.at[k]
        )
        for k in range(STENCIL)
    ]
    inputs = [
        pltpu.make_async_copy(source, target, input_sem.at[n])
        for n, (source, target) in enumerate(
            ((guess_hbm, guess), (sources_hbm, sources), (start_hbm, start), (retain_hbm, retain), (columns_hbm, columns_own), (columns_hbm, columns), (lists_hbm, lists))
        )
    ]
    for load in inputs + loads:
        load.start()

    def cells(p):
        return pl.ds(128 * p, 128)

    inbox[...] = jnp.zeros_like(inbox)
    barrier = pltpu.get_barrier_semaphore()
    for other in (before[1], before[2], after[1], after[2]):
        pl.semaphore_signal(barrier, inc=1, device_id={"tm": other}, device_id_type=MESH)
    for side in range(2):

        @pl.when(has[side])
        def _():
            pl.semaphore_signal(barrier, inc=1, device_id={"space": beside[side]}, device_id_type=MESH)

    @pl.when(is_far)
    def _():
        for d in range(3, n_tm - 2):
            pl.semaphore_signal(
                barrier, inc=1, device_id={"tm": lax.rem(tm + d, n_tm)}, device_id_type=MESH
            )

    @pl.when(is_far | is_relay)
    def _():
        pl.semaphore_signal(barrier, inc=1, device_id={"space": second}, device_id_type=MESH)

    for load in inputs[:2] + inputs[5:]:
        load.wait()
    for p in range(PAIRS):
        for f in range(C_DEV):
            guess_out[pl.ds(16 * f + p, 1), :] = guess[pl.ds(f, 1), cells(p)]
            forcing[pl.ds(64 * (4 + f) + 4 * p, 4), :] = sources[pl.ds(4 * f, 4), cells(p)]
    forcing[pl.ds(448, 64), :] = jnp.zeros((64, 128), jnp.float32)

    def to_slice(n, source, target, other):
        return pltpu.make_async_remote_copy(
            src_ref=source,
            dst_ref=target,
            send_sem=slice_send.at[n],
            recv_sem=slice_recv.at[n],
            device_id={"tm": other},
            device_id_type=MESH,
        )

    def interval(a):
        return forcing.at[pl.ds(64 * a, 64), :]

    slice_copies = [
        to_slice(0, guess_out.at[pl.ds(16, 32), :], guess_in.at[pl.ds(0, 32), :], after[2]),
        to_slice(1, guess_out.at[pl.ds(0, 16), :], guess_in.at[pl.ds(32, 16), :], after[1]),
        to_slice(2, interval(6), interval(0), after[2]),
        to_slice(3, interval(4), interval(1), after[1]),
        to_slice(4, interval(5), interval(2), after[1]),
        to_slice(5, interval(6), interval(3), after[1]),
    ]
    point_copy = to_slice(6, point_out, point_in, before[1])

    def halo_copy(slot, side):
        return pltpu.make_async_remote_copy(
            src_ref=outbox.at[slot, side],
            dst_ref=inbox.at[slot, 1 - side],
            send_sem=send_sem.at[slot, side],
            recv_sem=recv_sem.at[slot, 1 - side],
            device_id={"space": space + 2 * side - 1},
            device_id_type=MESH,
        )

    def twice(value):
        turned = pltpu.roll(value, BS, 1)
        return jnp.where(low, value, turned), jnp.where(low, turned, value)

    def in_parts(value):
        upper = value.astype(jnp.bfloat16).astype(jnp.float32)
        return jnp.where(top, upper, value - upper)

    def to_partner(n, source, target):
        return pltpu.make_async_remote_copy(
            src_ref=source,
            dst_ref=target,
            send_sem=far_send.at[n],
            recv_sem=far_recv.at[n],
            device_id={"space": partner},
            device_id_type=MESH,
        )

    def rows_of(slice_at):
        return far_coupling.at[pl.ds(pl.multiple_of(rows_each * slice_at, 8), rows_each), :]

    far_copies = [
        to_partner(0, piece, rows_of(tm)),
        to_partner(1, far_forcing_out, far_forcing),
        to_partner(2, far_cells_out, far_cells),
        to_partner(3, far_slots_out, far_slots_in),
    ]

    def spread_copy(d, slice_at):
        return pltpu.make_async_remote_copy(
            src_ref=rows_of(slice_at),
            dst_ref=rows_of(slice_at),
            send_sem=spread_send.at[d],
            recv_sem=spread_recv.at[d],
            device_id={"tm": lax.rem(tm + d, n_tm)},
            device_id_type=MESH,
        )

    def field_copy(step):
        slot = lax.rem(step, 2)
        return pltpu.make_async_remote_copy(
            src_ref=far_out.at[slot],
            dst_ref=far_in.at[step],
            send_sem=field_send.at[slot],
            recv_sem=field_recv.at[step],
            device_id={"space": partner},
            device_id_type=MESH,
        )

    def relay_copy(step):
        slot = lax.rem(step, 2)
        return pltpu.make_async_remote_copy(
            src_ref=outbox.at[slot, upper_half],
            dst_ref=relay_in.at[step],
            send_sem=relay_send.at[slot],
            recv_sem=relay_recv.at[step],
            device_id={"space": second},
            device_id_type=MESH,
        )

    def near(step, side):
        lower = has[0] & jnp.logical_not(across[0] & (step >= AHEAD))
        upper = has[1] & jnp.logical_not(across[1] & (step >= AHEAD))
        return ((side == 0) & lower) | ((side == 1) & upper)

    def fields_go(step):
        return (step >= AHEAD - 1) & (step < STEPS - 1)

    def store_twice(target, p, rows, value):
        half = lax.broadcasted_iota(jnp.int32, value.shape, 1) < BS
        turned = pltpu.roll(value, BS, 1)
        target[2 * p, rows, :] = jnp.where(half, value, turned)
        target[2 * p + 1, rows, :] = jnp.where(half, turned, value)

    def of_listed(blocks, q):
        values = [blocks[lists[upper_half, 2 * q + h]] for h in range(2)]
        return jnp.where(lax.broadcasted_iota(jnp.int32, values[0].shape, 1) < BS, *values)

    def arrive(step, p, value):
        begins = jnp.where(lax.rem(step, CF) == 0, 4 - C_DEV * tm - step // CF, -1)
        value = jnp.where(field == begins, start[pl.ds(p, 1), :], value)
        state[p] = value
        far_out[lax.rem(step, 2), pl.ds(4 * p, 4), :] = value[:4]
        doubled[2 * p], doubled[2 * p + 1] = twice(value)

    def send(step):
        slot = lax.rem(step, 2)

        @pl.when(is_far & fields_go(step))
        def _():
            field_copy(step).start()

        for side in (cross, 1 - cross):
            for q in range(HALO // 2):
                pair = jnp.where(low, doubled[lists[side, 2 * q]], doubled[lists[side, 2 * q + 1]])
                outbox[slot, side, pl.ds(4 * q, 4), :] = pair[:4]

            @pl.when(near(step, side))
            def _():
                halo_copy(slot, side).start()

        @pl.when(is_relay & fields_go(step))
        def _():
            relay_copy(step).start()

    @pl.when(is_far)
    def _():
        for load in loads:
            load.wait()
        for p in range(PAIRS):
            own_rows = pl.ds(pl.multiple_of(rows_each * tm, 8), rows_each)
            store_twice(block_rows, p, pl.ds(0, rows_each), coupling[own_rows, cells(p)])
        for q in range(HALO // 2):
            piece[:, cells(q)] = of_listed(block_rows, q)

    pl.semaphore_wait(
        barrier,
        4
        + has[0].astype(jnp.int32)
        + has[1].astype(jnp.int32)
        + (n_tm - 5) * is_far.astype(jnp.int32)
        + (is_far | is_relay).astype(jnp.int32),
    )


    for copy in slice_copies[:2]:
        copy.start()

    @pl.when(is_far)
    def _():
        far_copies[0].start()

    for copy in slice_copies[2:]:
        copy.start()
    for copy in slice_copies[:2]:
        copy.wait_recv()
    inputs[2].wait()
    for p in range(PAIRS):
        rows = [guess_in[pl.ds(16 * f + p, 1), :] for f in range(C_DEV)]
        rows.append(jnp.zeros((1, 128), jnp.float32))
        arrive(jnp.int32(0), p, jnp.concatenate(rows + rows, axis=0))
    send(jnp.int32(0))

    inputs[3].wait()
    inputs[4].wait()
    for p in range(PAIRS):
        retained[p] = jnp.where(top, retain[pl.ds(p, 1), :], 0.0)
    @pl.when(jnp.logical_not(is_far))
    def _():
        for load in loads:
            load.wait()

    for k in range(STENCIL):
        target, at, gap = (own_weights, 0, BS) if k == 0 else (weights, BS * (k - 1), REST)

        @pl.loop(0, BS // 16)
        def _(n, k=k, target=target, at=at, gap=gap):
            entries = coupling[pl.ds(pl.multiple_of(BS * k + 16 * n, 16), 16), :]
            upper = entries.astype(jnp.bfloat16)
            target[pl.ds(pl.multiple_of(at + 16 * n, 16), 16), :] = upper
            target[pl.ds(pl.multiple_of(at + gap + 16 * n, 16), 16), :] = (
                entries - upper.astype(jnp.float32)
            ).astype(jnp.bfloat16)

    def on_diagonal(product):
        return [
            jnp.where(
                low,
                product[16 * h : 16 * h + 8, 128 * h : 128 * h + 128],
                product[16 * h + 8 : 16 * h + 16, 128 * h : 128 * h + 128],
            )
            for h in range(2)
        ]

    def four_rows(value):
        return twice(in_parts(jnp.concatenate([value, value], axis=0)))

    def listed_by_partner(step):
        slot = lax.rem(step, 2)
        field_copy(step).wait_recv()
        relay_copy(step).wait_recv()
        for p in range(PAIRS):
            far_parts[2 * p], far_parts[2 * p + 1] = four_rows(far_in[step, pl.ds(4 * p, 4), :])
        for q in range(HALO // 2):
            at = NBLK + HALO * upper_half + 2 * q
            far_parts[at], far_parts[at + 1] = four_rows(relay_in[step, pl.ds(4 * q, 4), :])
            at = NBLK + HALO * (1 - upper_half) + 2 * q
            far_parts[at], far_parts[at + 1] = four_rows(outbox[slot, upper_half, pl.ds(4 * q, 4), :])
        begins = jnp.where(lax.rem(step + 1, CF) == 0, 4 - C_DEV * tm - (step + 1) // CF, -1)
        for g in range(HALO // 4):
            picked, firsts = [], []
            for j in range(4 * g, 4 * g + 4):
                firsts.append(far_parts[far_slots[j, STENCIL - 1]])
                rest = [
                    jnp.where(
                        low,
                        far_parts[far_slots[j, k]],
                        far_parts[far_slots[j, k + 1]],
                    )
                    for k in range(0, STENCIL - 1, 2)
                ]
                picked.append(jnp.concatenate(rest + rest + firsts[-1:], axis=1))
            product = jnp.dot(
                jnp.concatenate(picked, axis=0).astype(jnp.bfloat16),
                far_weights[:, 256 * g : 256 * g + 256],
                preferred_element_type=jnp.float32,
            )
            for h, pair in enumerate(on_diagonal(product)):
                q = 2 * g + h
                heat = far_forcing[pl.ds(step + 32 * q, 4, stride=CF), :]
                heat = jnp.concatenate([heat, jnp.zeros((4, 128), jnp.float32)], axis=0)
                now = jnp.where(low, firsts[2 * h], firsts[2 * h + 1])
                total = pair + far_cells[pl.ds(q, 1), :] * now + heat
                value = total + pltpu.roll(total, 4, 0)
                value = jnp.where(field == begins, far_cells[pl.ds(8 + q, 1), :], value)
                inbox[1 - slot, upper_half, pl.ds(4 * q, 4), :] = value[:4]

    def one_step(step, carry):
        slot = lax.rem(step, 2)

        @pl.when(step == 0)
        def _():
            for copy in slice_copies[2:]:
                copy.wait_recv()

        @pl.when((step == 0) & is_far)
        def _():
            for p in range(PAIRS):
                for a in range(8):
                    store_twice(block_forcing, p, pl.ds(4 * a, 4), forcing[pl.ds(64 * a + 4 * p, 4), :])
                for n, source in enumerate((retain, start)):
                    store_twice(block_cells, p, pl.ds(n, 1), source[pl.ds(p, 1), :])
            for q in range(HALO // 2):
                far_forcing_out[pl.ds(32 * q, 32), :] = of_listed(block_forcing, q)
                both = of_listed(block_cells, q)
                far_cells_out[pl.ds(q, 1), :] = both[0:1]
                far_cells_out[pl.ds(8 + q, 1), :] = both[1:2]
            wide = lax.broadcasted_iota(jnp.int32, (HALO, NBLK), 0)
            listed = jnp.zeros((HALO, NBLK), jnp.int32)
            for j in range(HALO):
                listed = jnp.where(wide == j, lists[upper_half, j], listed)
            chosen = listed == lax.broadcasted_iota(jnp.int32, (HALO, NBLK), 1)
            place_at = lax.broadcasted_iota(jnp.int32, (HALO, 128), 1)
            table = jnp.zeros((HALO, 128), jnp.int32)
            for k in range(STENCIL):
                if k < STENCIL - 1:
                    found = jnp.where(chosen, columns_own[pl.ds(k, 1), :], 0)
                else:
                    found = jnp.where(chosen, listed, 0)
                table = jnp.where(place_at == k, jnp.sum(found, axis=1, keepdims=True), table)
            far_slots_out[...] = table
            for copy in far_copies[1:]:
                copy.start()

        @pl.when((step == SPREAD) & is_far)
        def _():
            far_copies[0].wait_recv()
            for d in range(1, n_tm):
                spread_copy(d, tm).start()

        @pl.when((step == AHEAD - 1) & is_far)
        def _():
            for copy in far_copies[1:]:
                copy.wait_recv()
            slots = pltpu.make_async_copy(far_slots_in, far_slots, input_sem.at[7])
            slots.start()
            slots.wait()
            for d in range(1, n_tm):
                spread_copy(d, lax.rem(tm + n_tm - d, n_tm)).wait_recv()
            for k in range(STENCIL):
                at, gap = (2 * REST, BS) if k == 0 else (BS * (k - 1), REST)

                @pl.loop(0, BS // 16)
                def _(n, k=k, at=at, gap=gap):
                    entries = far_coupling[pl.ds(pl.multiple_of(BS * k + 16 * n, 16), 16), :]
                    upper = entries.astype(jnp.bfloat16)
                    far_weights[pl.ds(pl.multiple_of(at + 16 * n, 16), 16), :] = upper
                    far_weights[pl.ds(pl.multiple_of(at + gap + 16 * n, 16), 16), :] = (
                        entries - upper.astype(jnp.float32)
                    ).astype(jnp.bfloat16)

        @pl.when(step == 4 * CF)
        def _():
            for p in range(PAIRS):
                value = reached[p]
                values_out[pl.ds(0, 2), cells(p)] = value[1:3]
                point_out[pl.ds(p, 1), :] = value[0:1]
            point_copy.start()

        at = (step // CF) * 64 + lax.rem(step, CF)
        for g in range(GROUPS):
            own = []
            for b in range(4 * g, 4 * g + 4):
                own.append(in_parts(doubled[b]))
                parts[b] = own[-1]
            product = jnp.dot(
                jnp.concatenate(own, axis=0).astype(jnp.bfloat16),
                own_weights[:, 256 * g : 256 * g + 256],
                preferred_element_type=jnp.float32,
            )
            for h, pair in enumerate(on_diagonal(product)):
                p = 2 * g + h
                heat = forcing[pl.ds(at + 4 * p, 4, stride=64), :]
                heat = jnp.concatenate([heat, jnp.zeros((4, 128), jnp.float32)], axis=0)
                base[p] = pair + retained[p] * state[p] + heat

        for side in range(2):

            @pl.when(near(step, side))
            def _():
                halo_copy(slot, side).wait_send()

        @pl.when(is_far & fields_go(step))
        def _():
            field_copy(step).wait_send()

        @pl.when(is_relay & fields_go(step))
        def _():
            relay_copy(step).wait_send()

        @pl.when(is_far & (step >= AHEAD))
        def _():
            listed_by_partner(step - 1)

        for side in (1 - cross, cross):

            @pl.when(near(step, side))
            def _(side=side):
                halo_copy(slot, 1 - side).wait_recv()

            for q in range(HALO // 2):
                value = inbox[slot, side, pl.ds(4 * q, 4), :]
                n = NBLK + HALO * side + 2 * q
                parts[n], parts[n + 1] = four_rows(value)

        for g in range(GROUPS):
            picked = []
            for b in range(4 * g, 4 * g + 4):
                picked.append(
                    jnp.concatenate(
                        [
                            jnp.where(low, parts[columns[k, b]], parts[columns[k + 1, b]])
                            for k in range(0, STENCIL - 1, 2)
                        ],
                        axis=1,
                    )
                )
            left = jnp.concatenate(picked, axis=0).astype(jnp.bfloat16)
            product = jnp.dot(
                jnp.concatenate([left, left], axis=1),
                weights[:, 256 * g : 256 * g + 256],
                preferred_element_type=jnp.float32,
            )
            for h, pair in enumerate(on_diagonal(product)):
                total = base[2 * g + h] + pair
                value = total + pltpu.roll(total, 4, 0)
                reached[2 * g + h] = value
                arrive(step + 1, 2 * g + h, value)

        @pl.when(step < STEPS - 1)
        def _():
            send(step + 1)

        return carry

    lax.fori_loop(0, STEPS, one_step, 0)

    for copy in slice_copies:
        copy.wait_send()

    @pl.when(is_far)
    def _():
        for copy in far_copies:
            copy.wait_send()
        for d in range(1, n_tm):
            spread_copy(d, tm).wait_send()

    point_copy.wait()
    for p in range(PAIRS):
        values_out[pl.ds(2, 1), cells(p)] = point_in[pl.ds(p, 1), :]
        residual_out[:, cells(p)] = reached[p][:3] - values_out[:, cells(p)]


def body(n_tm, n_space, coupling, retain, sources, initial_guess, start_field, block_columns, send_lists):
    count = retain.shape[0]
    f32, bf16 = jnp.float32, jnp.bfloat16
    vmem = pl.BlockSpec(memory_space=pltpu.VMEM)
    return pl.pallas_call(
        functools.partial(kernel, n_tm, n_space),
        out_shape=(jax.ShapeDtypeStruct((C_DEV, count), f32),) * 2,
        in_specs=[pl.BlockSpec(memory_space=pl.ANY)] * 7,
        out_specs=(vmem, vmem),
        scratch_shapes=[
            pltpu.SMEM((STENCIL - 1, NBLK), jnp.int32),
            pltpu.SMEM((2, HALO), jnp.int32),
            pltpu.VMEM((PAIRS, 128), f32),
            pltpu.VMEM((C_DEV * CF, count), f32),
            pltpu.VMEM((C_DEV, count), f32),
            pltpu.VMEM((PAIRS, 128), f32),
            pltpu.VMEM((STENCIL * BS, count), f32),
            pltpu.VMEM((2 * BS, count), bf16),
            pltpu.VMEM((2 * REST, count), bf16),
            pltpu.VMEM((512, 128), f32),
            pltpu.VMEM((48, 128), f32),
            pltpu.VMEM((48, 128), f32),
            pltpu.VMEM((PAIRS, 8, 128), f32),
            pltpu.VMEM((PAIRS, 8, 128), f32),
            pltpu.VMEM((PAIRS, 8, 128), f32),
            pltpu.VMEM((NBLK, 8, 128), f32),
            pltpu.VMEM((NBLK + 2 * HALO, 8, 128), f32),
            pltpu.VMEM((PAIRS, 8, 128), f32),
            pltpu.VMEM((2, 2, 32, 128), f32),
            pltpu.VMEM((2, 2, 32, 128), f32),
            pltpu.VMEM((16, 128), f32),
            pltpu.VMEM((16, 128), f32),
            pltpu.VMEM((STENCIL * BS // n_tm, count // 2), f32),
            pltpu.VMEM((STENCIL * BS, count // 2), f32),
            pltpu.VMEM((2 * STENCIL * BS, count // 2), bf16),
            pltpu.VMEM((256, 128), f32),
            pltpu.VMEM((256, 128), f32),
            pltpu.VMEM((16, 128), f32),
            pltpu.VMEM((16, 128), f32),
            pltpu.VMEM((STENCIL - 1, NBLK), jnp.int32),
            pltpu.VMEM((HALO, 128), jnp.int32),
            pltpu.VMEM((HALO, 128), jnp.int32),
            pltpu.SMEM((HALO, 128), jnp.int32),
            pltpu.VMEM((NBLK, STENCIL * BS // n_tm, 128), f32),
            pltpu.VMEM((NBLK, 32, 128), f32),
            pltpu.VMEM((NBLK, 8, 128), f32),
            pltpu.VMEM((2, 64, 128), f32),
            pltpu.VMEM((STEPS, 64, 128), f32),
            pltpu.VMEM((STEPS, 32, 128), f32),
            pltpu.VMEM((NBLK + 2 * HALO, 8, 128), f32),
            pltpu.SemaphoreType.DMA((STENCIL,)),
            pltpu.SemaphoreType.DMA((8,)),
            pltpu.SemaphoreType.DMA((2, 2)),
            pltpu.SemaphoreType.DMA((2, 2)),
            pltpu.SemaphoreType.DMA((7,)),
            pltpu.SemaphoreType.DMA((7,)),
            pltpu.SemaphoreType.DMA((4,)),
            pltpu.SemaphoreType.DMA((4,)),
            pltpu.SemaphoreType.DMA((n_tm,)),
            pltpu.SemaphoreType.DMA((n_tm,)),
            pltpu.SemaphoreType.DMA((2,)),
            pltpu.SemaphoreType.DMA((STEPS,)),
            pltpu.SemaphoreType.DMA((2,)),
            pltpu.SemaphoreType.DMA((STEPS,)),
        ],
        compiler_params=pltpu.CompilerParams(
            collective_id=0, has_side_effects=True, vmem_limit_bytes=60 * 2**20
        ),
    )(
        send_lists,
        coupling,
        retain.reshape(PAIRS, 128),
        sources,
        initial_guess,
        start_field.reshape(PAIRS, 128),
        block_columns.T,
    )


def solution(mesh):
    placed = (
        P(None, "space"),
        P("space"),
        P("tm", "space"),
        P("tm", "space"),
        P("space"),
        P("space", None),
        P("space", None),
    )
    return jax.shard_map(
        functools.partial(body, mesh.shape["tm"], mesh.shape["space"]),
        mesh=mesh,
        in_specs=placed,
        out_specs=(P("tm", "space"), P("tm", "space")),
        check_vma=False,
    )
```

```python
import functools

import jax
import jax.numpy as jnp
from jax import lax
from jax.experimental import pallas as pl
from jax.experimental.pallas import tpu as pltpu
from jax.sharding import PartitionSpec as P

BS = 64
STENCIL = 7
NBLK = 32
CF = 4
C_DEV = 3
SWEEPS = 5
HALO = 16
PAIRS = NBLK // 2
GROUPS = NBLK // 4
STEPS = SWEEPS * CF
REST = (STENCIL - 1) * BS
ROW = 8
SPREAD = 1
AHEAD = 3
MESH = pl.DeviceIdType.MESH


def kernel(
    n_tm,
    n_space,
    lists_hbm,
    coupling_hbm,
    retain_hbm,
    sources_hbm,
    guess_hbm,
    start_hbm,
    columns_hbm,
    values_out,
    residual_out,
    columns,
    lists,
    retain,
    sources,
    guess,
    start,
    coupling,
    own_weights,
    weights,
    forcing,
    guess_out,
    guess_in,
    retained,
    state,
    reached,
    doubled,
    parts,
    base,
    outbox,
    inbox,
    point_out,
    point_in,
    piece,
    far_coupling,
    far_weights,
    far_forcing_out,
    far_forcing,
    far_cells_out,
    far_cells,
    columns_own,
    far_slots_out,
    far_slots_in,
    far_slots,
    block_rows,
    block_forcing,
    block_cells,
    far_out,
    far_in,
    relay_in,
    far_parts,
    coupling_sem,
    input_sem,
    send_sem,
    recv_sem,
    slice_send,
    slice_recv,
    far_send,
    far_recv,
    spread_send,
    spread_recv,
    field_send,
    field_recv,
    relay_send,
    relay_recv,
):
    tm, space = lax.axis_index("tm"), lax.axis_index("space")
    before = [lax.rem(tm + n_tm - d, n_tm) for d in range(3)]
    after = [lax.rem(tm + d, n_tm) for d in range(3)]
    has = (space > 0, space < n_space - 1)
    beside = (space - 1, space + 1)
    place = lax.rem(space, ROW)
    across = ((place == 0) & has[0], (place == ROW - 1) & has[1])
    is_far = across[0] | across[1]
    is_relay = ((place == 1) & (space > 1)) | ((place == ROW - 2) & (space < n_space - 2))
    upper_half = (place >= ROW // 2).astype(jnp.int32)
    partner = space + 2 * upper_half - 1
    second = space + 4 * upper_half - 2
    rows_each = STENCIL * BS // n_tm
    cross = lax.rem(space, 2)

    lane = lax.broadcasted_iota(jnp.int32, (8, 128), 1)
    row = lax.broadcasted_iota(jnp.int32, (8, 128), 0)
    low, top = lane < BS, row < 4
    field = lax.rem(row, 4)

    loads = [
        pltpu.make_async_copy(
            coupling_hbm.at[pl.ds(BS * k, BS), :], coupling.at[pl.ds(BS * k, BS), :], coupling_sem.at[k]
        )
        for k in range(STENCIL)
    ]
    inputs = [
        pltpu.make_async_copy(source, target, input_sem.at[n])
        for n, (source, target) in enumerate(
            ((guess_hbm, guess), (sources_hbm, sources), (start_hbm, start), (retain_hbm, retain), (columns_hbm, columns_own), (columns_hbm, columns), (lists_hbm, lists))
        )
    ]
    for load in inputs + loads:
        load.start()

    def cells(p):
        return pl.ds(128 * p, 128)

    inbox[...] = jnp.zeros_like(inbox)
    barrier = pltpu.get_barrier_semaphore()
    for other in (before[1], before[2], after[1], after[2]):
        pl.semaphore_signal(barrier, inc=1, device_id={"tm": other}, device_id_type=MESH)
    for side in range(2):

        @pl.when(has[side])
        def _():
            pl.semaphore_signal(barrier, inc=1, device_id={"space": beside[side]}, device_id_type=MESH)

    @pl.when(is_far)
    def _():
        for d in range(3, n_tm - 2):
            pl.semaphore_signal(
                barrier, inc=1, device_id={"tm": lax.rem(tm + d, n_tm)}, device_id_type=MESH
            )

    @pl.when(is_far | is_relay)
    def _():
        pl.semaphore_signal(barrier, inc=1, device_id={"space": second}, device_id_type=MESH)

    for load in inputs[:2] + inputs[5:]:
        load.wait()
    for p in range(PAIRS):
        for f in range(C_DEV):
            guess_out[pl.ds(16 * f + p, 1), :] = guess[pl.ds(f, 1), cells(p)]
            forcing[pl.ds(64 * (4 + f) + 4 * p, 4), :] = sources[pl.ds(4 * f, 4), cells(p)]
    forcing[pl.ds(448, 64), :] = jnp.zeros((64, 128), jnp.float32)

    def to_slice(n, source, target, other):
        return pltpu.make_async_remote_copy(
            src_ref=source,
            dst_ref=target,
            send_sem=slice_send.at[n],
            recv_sem=slice_recv.at[n],
            device_id={"tm": other},
            device_id_type=MESH,
        )

    def interval(a):
        return forcing.at[pl.ds(64 * a, 64), :]

    slice_copies = [
        to_slice(0, guess_out.at[pl.ds(16, 32), :], guess_in.at[pl.ds(0, 32), :], after[2]),
        to_slice(1, guess_out.at[pl.ds(0, 16), :], guess_in.at[pl.ds(32, 16), :], after[1]),
        to_slice(2, interval(6), interval(0), after[2]),
        to_slice(3, interval(4), interval(1), after[1]),
        to_slice(4, interval(5), interval(2), after[1]),
        to_slice(5, interval(6), interval(3), after[1]),
    ]
    point_copy = to_slice(6, point_out, point_in, before[1])

    def halo_copy(slot, side):
        return pltpu.make_async_remote_copy(
            src_ref=outbox.at[slot, side],
            dst_ref=inbox.at[slot, 1 - side],
            send_sem=send_sem.at[slot, side],
            recv_sem=recv_sem.at[slot, 1 - side],
            device_id={"space": space + 2 * side - 1},
            device_id_type=MESH,
        )

    def twice(value):
        turned = pltpu.roll(value, BS, 1)
        return jnp.where(low, value, turned), jnp.where(low, turned, value)

    def in_parts(value):
        upper = value.astype(jnp.bfloat16).astype(jnp.float32)
        return jnp.where(top, upper, value - upper)

    def to_partner(n, source, target):
        return pltpu.make_async_remote_copy(
            src_ref=source,
            dst_ref=target,
            send_sem=far_send.at[n],
            recv_sem=far_recv.at[n],
            device_id={"space": partner},
            device_id_type=MESH,
        )

    def rows_of(slice_at):
        return far_coupling.at[pl.ds(pl.multiple_of(rows_each * slice_at, 8), rows_each), :]

    far_copies = [
        to_partner(0, piece, rows_of(tm)),
        to_partner(1, far_forcing_out, far_forcing),
        to_partner(2, far_cells_out, far_cells),
        to_partner(3, far_slots_out, far_slots_in),
    ]

    def spread_copy(d, slice_at):
        return pltpu.make_async_remote_copy(
            src_ref=rows_of(slice_at),
            dst_ref=rows_of(slice_at),
            send_sem=spread_send.at[d],
            recv_sem=spread_recv.at[d],
            device_id={"tm": lax.rem(tm + d, n_tm)},
            device_id_type=MESH,
        )

    def field_copy(step):
        slot = lax.rem(step, 2)
        return pltpu.make_async_remote_copy(
            src_ref=far_out.at[slot],
            dst_ref=far_in.at[step],
            send_sem=field_send.at[slot],
            recv_sem=field_recv.at[step],
            device_id={"space": partner},
            device_id_type=MESH,
        )

    def relay_copy(step):
        slot = lax.rem(step, 2)
        return pltpu.make_async_remote_copy(
            src_ref=outbox.at[slot, upper_half],
            dst_ref=relay_in.at[step],
            send_sem=relay_send.at[slot],
            recv_sem=relay_recv.at[step],
            device_id={"space": second},
            device_id_type=MESH,
        )

    def near(step, side):
        lower = has[0] & jnp.logical_not(across[0] & (step >= AHEAD))
        upper = has[1] & jnp.logical_not(across[1] & (step >= AHEAD))
        return ((side == 0) & lower) | ((side == 1) & upper)

    def fields_go(step):
        return (step >= AHEAD - 1) & (step < STEPS - 1)

    def store_twice(target, p, rows, value):
        half = lax.broadcasted_iota(jnp.int32, value.shape, 1) < BS
        turned = pltpu.roll(value, BS, 1)
        target[2 * p, rows, :] = jnp.where(half, value, turned)
        target[2 * p + 1, rows, :] = jnp.where(half, turned, value)

    def of_listed(blocks, q):
        values = [blocks[lists[upper_half, 2 * q + h]] for h in range(2)]
        return jnp.where(lax.broadcasted_iota(jnp.int32, values[0].shape, 1) < BS, *values)

    def arrive(step, p, value):
        begins = jnp.where(lax.rem(step, CF) == 0, 4 - C_DEV * tm - step // CF, -1)
        value = jnp.where(field == begins, start[pl.ds(p, 1), :], value)
        state[p] = value
        far_out[lax.rem(step, 2), pl.ds(4 * p, 4), :] = value[:4]
        doubled[2 * p], doubled[2 * p + 1] = twice(value)

    def send(step):
        slot = lax.rem(step, 2)

        @pl.when(is_far & fields_go(step))
        def _():
            field_copy(step).start()

        for side in (cross, 1 - cross):
            for q in range(HALO // 2):
                pair = jnp.where(low, doubled[lists[side, 2 * q]], doubled[lists[side, 2 * q + 1]])
                outbox[slot, side, pl.ds(4 * q, 4), :] = pair[:4]

            @pl.when(near(step, side))
            def _():
                halo_copy(slot, side).start()

        @pl.when(is_relay & fields_go(step))
        def _():
            relay_copy(step).start()

    @pl.when(is_far)
    def _():
        for load in loads:
            load.wait()
        for p in range(PAIRS):
            own_rows = pl.ds(pl.multiple_of(rows_each * tm, 8), rows_each)
            store_twice(block_rows, p, pl.ds(0, rows_each), coupling[own_rows, cells(p)])
        for q in range(HALO // 2):
            piece[:, cells(q)] = of_listed(block_rows, q)

    pl.semaphore_wait(
        barrier,
        4
        + has[0].astype(jnp.int32)
        + has[1].astype(jnp.int32)
        + (n_tm - 5) * is_far.astype(jnp.int32)
        + (is_far | is_relay).astype(jnp.int32),
    )


    for copy in slice_copies[:2]:
        copy.start()

    @pl.when(is_far)
    def _():
        far_copies[0].start()

    for copy in slice_copies[2:]:
        copy.start()
    for copy in slice_copies[:2]:
        copy.wait_recv()
    inputs[2].wait()
    for p in range(PAIRS):
        rows = [guess_in[pl.ds(16 * f + p, 1), :] for f in range(C_DEV)]
        rows.append(jnp.zeros((1, 128), jnp.float32))
        arrive(jnp.int32(0), p, jnp.concatenate(rows + rows, axis=0))
    send(jnp.int32(0))

    inputs[3].wait()
    inputs[4].wait()
    for p in range(PAIRS):
        retained[p] = jnp.where(top, retain[pl.ds(p, 1), :], 0.0)
    @pl.when(jnp.logical_not(is_far))
    def _():
        for load in loads:
            load.wait()

    for k in range(STENCIL):
        target, at, gap = (own_weights, 0, BS) if k == 0 else (weights, BS * (k - 1), REST)

        @pl.loop(0, BS // 16)
        def _(n, k=k, target=target, at=at, gap=gap):
            entries = coupling[pl.ds(pl.multiple_of(BS * k + 16 * n, 16), 16), :]
            upper = entries.astype(jnp.bfloat16)
            target[pl.ds(pl.multiple_of(at + 16 * n, 16), 16), :] = upper
            target[pl.ds(pl.multiple_of(at + gap + 16 * n, 16), 16), :] = (
                entries - upper.astype(jnp.float32)
            ).astype(jnp.bfloat16)

    def on_diagonal(product):
        return [
            jnp.where(
                low,
                product[16 * h : 16 * h + 8, 128 * h : 128 * h + 128],
                product[16 * h + 8 : 16 * h + 16, 128 * h : 128 * h + 128],
            )
            for h in range(2)
        ]

    def four_rows(value):
        return twice(in_parts(jnp.concatenate([value, value], axis=0)))

    def listed_by_partner(step):
        slot = lax.rem(step, 2)
        field_copy(step).wait_recv()
        relay_copy(step).wait_recv()
        for p in range(PAIRS):
            far_parts[2 * p], far_parts[2 * p + 1] = four_rows(far_in[step, pl.ds(4 * p, 4), :])
        for q in range(HALO // 2):
            at = NBLK + HALO * upper_half + 2 * q
            far_parts[at], far_parts[at + 1] = four_rows(relay_in[step, pl.ds(4 * q, 4), :])
            at = NBLK + HALO * (1 - upper_half) + 2 * q
            far_parts[at], far_parts[at + 1] = four_rows(outbox[slot, upper_half, pl.ds(4 * q, 4), :])
        begins = jnp.where(lax.rem(step + 1, CF) == 0, 4 - C_DEV * tm - (step + 1) // CF, -1)
        for g in range(HALO // 4):
            picked, firsts = [], []
            for j in range(4 * g, 4 * g + 4):
                firsts.append(far_parts[far_slots[j, STENCIL - 1]])
                rest = [
                    jnp.where(
                        low,
                        far_parts[far_slots[j, k]],
                        far_parts[far_slots[j, k + 1]],
                    )
                    for k in range(0, STENCIL - 1, 2)
                ]
                picked.append(jnp.concatenate(rest + rest + firsts[-1:], axis=1))
            product = jnp.dot(
                jnp.concatenate(picked, axis=0).astype(jnp.bfloat16),
                far_weights[:, 256 * g : 256 * g + 256],
                preferred_element_type=jnp.float32,
            )
            for h, pair in enumerate(on_diagonal(product)):
                q = 2 * g + h
                heat = far_forcing[pl.ds(step + 32 * q, 4, stride=CF), :]
                heat = jnp.concatenate([heat, jnp.zeros((4, 128), jnp.float32)], axis=0)
                now = jnp.where(low, firsts[2 * h], firsts[2 * h + 1])
                total = pair + far_cells[pl.ds(q, 1), :] * now + heat
                value = total + pltpu.roll(total, 4, 0)
                value = jnp.where(field == begins, far_cells[pl.ds(8 + q, 1), :], value)
                inbox[1 - slot, upper_half, pl.ds(4 * q, 4), :] = value[:4]

    def one_step(step, carry):
        slot = lax.rem(step, 2)

        @pl.when(step == 0)
        def _():
            for copy in slice_copies[2:]:
                copy.wait_recv()

        @pl.when((step == 0) & is_far)
        def _():
            for p in range(PAIRS):
                for a in range(8):
                    store_twice(block_forcing, p, pl.ds(4 * a, 4), forcing[pl.ds(64 * a + 4 * p, 4), :])
                for n, source in enumerate((retain, start)):
                    store_twice(block_cells, p, pl.ds(n, 1), source[pl.ds(p, 1), :])
            for q in range(HALO // 2):
                far_forcing_out[pl.ds(32 * q, 32), :] = of_listed(block_forcing, q)
                both = of_listed(block_cells, q)
                far_cells_out[pl.ds(q, 1), :] = both[0:1]
                far_cells_out[pl.ds(8 + q, 1), :] = both[1:2]
            wide = lax.broadcasted_iota(jnp.int32, (HALO, NBLK), 0)
            listed = jnp.zeros((HALO, NBLK), jnp.int32)
            for j in range(HALO):
                listed = jnp.where(wide == j, lists[upper_half, j], listed)
            chosen = listed == lax.broadcasted_iota(jnp.int32, (HALO, NBLK), 1)
            place_at = lax.broadcasted_iota(jnp.int32, (HALO, 128), 1)
            table = jnp.zeros((HALO, 128), jnp.int32)
            for k in range(STENCIL):
                if k < STENCIL - 1:
                    found = jnp.where(chosen, columns_own[pl.ds(k, 1), :], 0)
                else:
                    found = jnp.where(chosen, listed, 0)
                table = jnp.where(place_at == k, jnp.sum(found, axis=1, keepdims=True), table)
            far_slots_out[...] = table
            for copy in far_copies[1:]:
                copy.start()

        @pl.when((step == SPREAD) & is_far)
        def _():
            far_copies[0].wait_recv()
            for d in range(1, n_tm):
                spread_copy(d, tm).start()

        @pl.when((step == AHEAD - 1) & is_far)
        def _():
            for copy in far_copies[1:]:
                copy.wait_recv()
            slots = pltpu.make_async_copy(far_slots_in, far_slots, input_sem.at[7])
            slots.start()
            slots.wait()
            for d in range(1, n_tm):
                spread_copy(d, lax.rem(tm + n_tm - d, n_tm)).wait_recv()
            for k in range(STENCIL):
                at, gap = (2 * REST, BS) if k == 0 else (BS * (k - 1), REST)

                @pl.loop(0, BS // 16)
                def _(n, k=k, at=at, gap=gap):
                    entries = far_coupling[pl.ds(pl.multiple_of(BS * k + 16 * n, 16), 16), :]
                    upper = entries.astype(jnp.bfloat16)
                    far_weights[pl.ds(pl.multiple_of(at + 16 * n, 16), 16), :] = upper
                    far_weights[pl.ds(pl.multiple_of(at + gap + 16 * n, 16), 16), :] = (
                        entries - upper.astype(jnp.float32)
                    ).astype(jnp.bfloat16)

        @pl.when(step == 4 * CF)
        def _():
            for p in range(PAIRS):
                value = reached[p]
                values_out[pl.ds(0, 2), cells(p)] = value[1:3]
                point_out[pl.ds(p, 1), :] = value[0:1]
            point_copy.start()

        at = (step // CF) * 64 + lax.rem(step, CF)
        for g in range(GROUPS):
            own = []
            for b in range(4 * g, 4 * g + 4):
                own.append(in_parts(doubled[b]))
                parts[b] = own[-1]
            product = jnp.dot(
                jnp.concatenate(own, axis=0).astype(jnp.bfloat16),
                own_weights[:, 256 * g : 256 * g + 256],
                preferred_element_type=jnp.float32,
            )
            for h, pair in enumerate(on_diagonal(product)):
                p = 2 * g + h
                heat = forcing[pl.ds(at + 4 * p, 4, stride=64), :]
                heat = jnp.concatenate([heat, jnp.zeros((4, 128), jnp.float32)], axis=0)
                base[p] = pair + retained[p] * state[p] + heat

        for side in range(2):

            @pl.when(near(step, side))
            def _():
                halo_copy(slot, side).wait_send()

        @pl.when(is_far & fields_go(step))
        def _():
            field_copy(step).wait_send()

        @pl.when(is_relay & fields_go(step))
        def _():
            relay_copy(step).wait_send()

        @pl.when(is_far & (step >= AHEAD))
        def _():
            listed_by_partner(step - 1)

        for side in (1 - cross, cross):

            @pl.when(near(step, side))
            def _(side=side):
                halo_copy(slot, 1 - side).wait_recv()

            for q in range(HALO // 2):
                value = inbox[slot, side, pl.ds(4 * q, 4), :]
                n = NBLK + HALO * side + 2 * q
                parts[n], parts[n + 1] = four_rows(value)

        for g in range(GROUPS):
            picked = []
            for b in range(4 * g, 4 * g + 4):
                picked.append(
                    jnp.concatenate(
                        [
                            jnp.where(low, parts[columns[k, b]], parts[columns[k + 1, b]])
                            for k in range(0, STENCIL - 1, 2)
                        ],
                        axis=1,
                    )
                )
            left = jnp.concatenate(picked, axis=0).astype(jnp.bfloat16)
            product = jnp.dot(
                jnp.concatenate([left, left], axis=1),
                weights[:, 256 * g : 256 * g + 256],
                preferred_element_type=jnp.float32,
            )
            for h, pair in enumerate(on_diagonal(product)):
                total = base[2 * g + h] + pair
                value = total + pltpu.roll(total, 4, 0)
                reached[2 * g + h] = value
                arrive(step + 1, 2 * g + h, value)

        @pl.when(step < STEPS - 1)
        def _():
            send(step + 1)

        return carry

    lax.fori_loop(0, STEPS, one_step, 0)

    for copy in slice_copies:
        copy.wait_send()

    @pl.when(is_far)
    def _():
        for copy in far_copies:
            copy.wait_send()
        for d in range(1, n_tm):
            spread_copy(d, tm).wait_send()

    point_copy.wait()
    for p in range(PAIRS):
        values_out[pl.ds(2, 1), cells(p)] = point_in[pl.ds(p, 1), :]
        residual_out[:, cells(p)] = reached[p][:3] - values_out[:, cells(p)]


def body(n_tm, n_space, coupling, retain, sources, initial_guess, start_field, block_columns, send_lists):
    count = retain.shape[0]
    f32, bf16 = jnp.float32, jnp.bfloat16
    vmem = pl.BlockSpec(memory_space=pltpu.VMEM)
    return pl.pallas_call(
        functools.partial(kernel, n_tm, n_space),
        out_shape=(jax.ShapeDtypeStruct((C_DEV, count), f32),) * 2,
        in_specs=[pl.BlockSpec(memory_space=pl.ANY)] * 7,
        out_specs=(vmem, vmem),
        scratch_shapes=[
            pltpu.SMEM((STENCIL - 1, NBLK), jnp.int32),
            pltpu.SMEM((2, HALO), jnp.int32),
            pltpu.VMEM((PAIRS, 128), f32),
            pltpu.VMEM((C_DEV * CF, count), f32),
            pltpu.VMEM((C_DEV, count), f32),
            pltpu.VMEM((PAIRS, 128), f32),
            pltpu.VMEM((STENCIL * BS, count), f32),
            pltpu.VMEM((2 * BS, count), bf16),
            pltpu.VMEM((2 * REST, count), bf16),
            pltpu.VMEM((512, 128), f32),
            pltpu.VMEM((48, 128), f32),
            pltpu.VMEM((48, 128), f32),
            pltpu.VMEM((PAIRS, 8, 128), f32),
            pltpu.VMEM((PAIRS, 8, 128), f32),
            pltpu.VMEM((PAIRS, 8, 128), f32),
            pltpu.VMEM((NBLK, 8, 128), f32),
            pltpu.VMEM((NBLK + 2 * HALO, 8, 128), f32),
            pltpu.VMEM((PAIRS, 8, 128), f32),
            pltpu.VMEM((2, 2, 32, 128), f32),
            pltpu.VMEM((2, 2, 32, 128), f32),
            pltpu.VMEM((16, 128), f32),
            pltpu.VMEM((16, 128), f32),
            pltpu.VMEM((STENCIL * BS // n_tm, count // 2), f32),
            pltpu.VMEM((STENCIL * BS, count // 2), f32),
            pltpu.VMEM((2 * STENCIL * BS, count // 2), bf16),
            pltpu.VMEM((256, 128), f32),
            pltpu.VMEM((256, 128), f32),
            pltpu.VMEM((16, 128), f32),
            pltpu.VMEM((16, 128), f32),
            pltpu.VMEM((STENCIL - 1, NBLK), jnp.int32),
            pltpu.VMEM((HALO, 128), jnp.int32),
            pltpu.VMEM((HALO, 128), jnp.int32),
            pltpu.SMEM((HALO, 128), jnp.int32),
            pltpu.VMEM((NBLK, STENCIL * BS // n_tm, 128), f32),
            pltpu.VMEM((NBLK, 32, 128), f32),
            pltpu.VMEM((NBLK, 8, 128), f32),
            pltpu.VMEM((2, 64, 128), f32),
            pltpu.VMEM((STEPS, 64, 128), f32),
            pltpu.VMEM((STEPS, 32, 128), f32),
            pltpu.VMEM((NBLK + 2 * HALO, 8, 128), f32),
            pltpu.SemaphoreType.DMA((STENCIL,)),
            pltpu.SemaphoreType.DMA((8,)),
            pltpu.SemaphoreType.DMA((2, 2)),
            pltpu.SemaphoreType.DMA((2, 2)),
            pltpu.SemaphoreType.DMA((7,)),
            pltpu.SemaphoreType.DMA((7,)),
            pltpu.SemaphoreType.DMA((4,)),
            pltpu.SemaphoreType.DMA((4,)),
            pltpu.SemaphoreType.DMA((n_tm,)),
            pltpu.SemaphoreType.DMA((n_tm,)),
            pltpu.SemaphoreType.DMA((2,)),
            pltpu.SemaphoreType.DMA((STEPS,)),
            pltpu.SemaphoreType.DMA((2,)),
            pltpu.SemaphoreType.DMA((STEPS,)),
        ],
        compiler_params=pltpu.CompilerParams(
            collective_id=0, has_side_effects=True, vmem_limit_bytes=60 * 2**20
        ),
    )(
        send_lists,
        coupling,
        retain.reshape(PAIRS, 128),
        sources,
        initial_guess,
        start_field.reshape(PAIRS, 128),
        block_columns.T,
    )


def solution(mesh):
    placed = (
        P(None, "space"),
        P("space"),
        P("tm", "space"),
        P("tm", "space"),
        P("space"),
        P("space", None),
        P("space", None),
    )
    return jax.shard_map(
        functools.partial(body, mesh.shape["tm"], mesh.shape["space"]),
        mesh=mesh,
        in_specs=placed,
        out_specs=(P("tm", "space"), P("tm", "space")),
        check_vma=False,
    )
```

```python
import functools

import jax
import jax.numpy as jnp
from jax import lax
from jax.experimental import pallas as pl
from jax.experimental.pallas import tpu as pltpu
from jax.sharding import PartitionSpec as P

BS = 64
STENCIL = 7
NBLK = 32
CF = 4
C_DEV = 3
SWEEPS = 5
HALO = 16
PAIRS = NBLK // 2
GROUPS = NBLK // 4
STEPS = SWEEPS * CF
REST = (STENCIL - 1) * BS
ROW = 8
SPREAD = 1
AHEAD = 3
MESH = pl.DeviceIdType.MESH


def kernel(
    n_tm,
    n_space,
    lists_hbm,
    coupling_hbm,
    retain_hbm,
    sources_hbm,
    guess_hbm,
    start_hbm,
    columns_hbm,
    values_out,
    residual_out,
    columns,
    lists,
    retain,
    sources,
    guess,
    start,
    coupling,
    own_weights,
    weights,
    forcing,
    guess_out,
    guess_in,
    retained,
    state,
    reached,
    doubled,
    parts,
    base,
    outbox,
    inbox,
    point_out,
    point_in,
    piece,
    far_coupling,
    far_weights,
    far_forcing_out,
    far_forcing,
    far_cells_out,
    far_cells,
    columns_own,
    far_slots_out,
    far_slots_in,
    far_slots,
    block_rows,
    block_forcing,
    block_cells,
    far_out,
    far_in,
    relay_in,
    far_parts,
    coupling_sem,
    input_sem,
    send_sem,
    recv_sem,
    slice_send,
    slice_recv,
    far_send,
    far_recv,
    spread_send,
    spread_recv,
    field_send,
    field_recv,
    relay_send,
    relay_recv,
):
    tm, space = lax.axis_index("tm"), lax.axis_index("space")
    before = [lax.rem(tm + n_tm - d, n_tm) for d in range(3)]
    after = [lax.rem(tm + d, n_tm) for d in range(3)]
    has = (space > 0, space < n_space - 1)
    beside = (space - 1, space + 1)
    place = lax.rem(space, ROW)
    across = ((place == 0) & has[0], (place == ROW - 1) & has[1])
    is_far = across[0] | across[1]
    is_relay = ((place == 1) & (space > 1)) | ((place == ROW - 2) & (space < n_space - 2))
    upper_half = (place >= ROW // 2).astype(jnp.int32)
    partner = space + 2 * upper_half - 1
    second = space + 4 * upper_half - 2
    rows_each = STENCIL * BS // n_tm
    cross = lax.rem(space, 2)

    lane = lax.broadcasted_iota(jnp.int32, (8, 128), 1)
    row = lax.broadcasted_iota(jnp.int32, (8, 128), 0)
    low, top = lane < BS, row < 4
    field = lax.rem(row, 4)

    loads = [
        pltpu.make_async_copy(
            coupling_hbm.at[pl.ds(BS * k, BS), :], coupling.at[pl.ds(BS * k, BS), :], coupling_sem.at[k]
        )
        for k in range(STENCIL)
    ]
    inputs = [
        pltpu.make_async_copy(source, target, input_sem.at[n])
        for n, (source, target) in enumerate(
            ((guess_hbm, guess), (sources_hbm, sources), (start_hbm, start), (retain_hbm, retain), (columns_hbm, columns_own), (columns_hbm, columns), (lists_hbm, lists))
        )
    ]
    for load in inputs + loads:
        load.start()

    def cells(p):
        return pl.ds(128 * p, 128)

    inbox[...] = jnp.zeros_like(inbox)
    outbox[...] = jnp.zeros_like(outbox)
    for step in range(STEPS):
        relay_in[step, pl.ds(24, 8), :] = jnp.zeros((8, 128), jnp.float32)
    barrier = pltpu.get_barrier_semaphore()
    for other in (before[1], before[2], after[1], after[2]):
        pl.semaphore_signal(barrier, inc=1, device_id={"tm": other}, device_id_type=MESH)
    for side in range(2):

        @pl.when(has[side])
        def _():
            pl.semaphore_signal(barrier, inc=1, device_id={"space": beside[side]}, device_id_type=MESH)

    @pl.when(is_far)
    def _():
        for d in range(3, n_tm - 2):
            pl.semaphore_signal(
                barrier, inc=1, device_id={"tm": lax.rem(tm + d, n_tm)}, device_id_type=MESH
            )

    @pl.when(is_far | is_relay)
    def _():
        pl.semaphore_signal(barrier, inc=1, device_id={"space": second}, device_id_type=MESH)

    for load in inputs[:2] + inputs[5:]:
        load.wait()
    for p in range(PAIRS):
        for f in range(C_DEV):
            guess_out[pl.ds(16 * f + p, 1), :] = guess[pl.ds(f, 1), cells(p)]
            forcing[pl.ds(64 * (4 + f) + 4 * p, 4), :] = sources[pl.ds(4 * f, 4), cells(p)]
    forcing[pl.ds(448, 64), :] = jnp.zeros((64, 128), jnp.float32)

    def to_slice(n, source, target, other):
        return pltpu.make_async_remote_copy(
            src_ref=source,
            dst_ref=target,
            send_sem=slice_send.at[n],
            recv_sem=slice_recv.at[n],
            device_id={"tm": other},
            device_id_type=MESH,
        )

    def interval(a):
        return forcing.at[pl.ds(64 * a, 64), :]

    slice_copies = [
        to_slice(0, guess_out.at[pl.ds(16, 32), :], guess_in.at[pl.ds(0, 32), :], after[2]),
        to_slice(1, guess_out.at[pl.ds(0, 16), :], guess_in.at[pl.ds(32, 16), :], after[1]),
        to_slice(2, interval(6), interval(0), after[2]),
        to_slice(3, interval(4), interval(1), after[1]),
        to_slice(4, interval(5), interval(2), after[1]),
        to_slice(5, interval(6), interval(3), after[1]),
    ]
    point_copy = to_slice(6, point_out, point_in, before[1])

    def halo_copy(slot, side):
        return pltpu.make_async_remote_copy(
            src_ref=outbox.at[slot, side, pl.ds(0, 24), :],
            dst_ref=inbox.at[slot, 1 - side, pl.ds(0, 24), :],
            send_sem=send_sem.at[slot, side],
            recv_sem=recv_sem.at[slot, 1 - side],
            device_id={"space": space + 2 * side - 1},
            device_id_type=MESH,
        )

    def twice(value):
        turned = pltpu.roll(value, BS, 1)
        return jnp.where(low, value, turned), jnp.where(low, turned, value)

    def in_parts(value):
        upper = value.astype(jnp.bfloat16).astype(jnp.float32)
        return jnp.where(top, upper, value - upper)

    def to_partner(n, source, target):
        return pltpu.make_async_remote_copy(
            src_ref=source,
            dst_ref=target,
            send_sem=far_send.at[n],
            recv_sem=far_recv.at[n],
            device_id={"space": partner},
            device_id_type=MESH,
        )

    def rows_of(slice_at):
        return far_coupling.at[pl.ds(pl.multiple_of(rows_each * slice_at, 8), rows_each), :]

    far_copies = [
        to_partner(0, piece, rows_of(tm)),
        to_partner(1, far_forcing_out, far_forcing),
        to_partner(2, far_cells_out, far_cells),
        to_partner(3, far_slots_out, far_slots_in),
    ]

    def spread_copy(d, slice_at):
        return pltpu.make_async_remote_copy(
            src_ref=rows_of(slice_at),
            dst_ref=rows_of(slice_at),
            send_sem=spread_send.at[d],
            recv_sem=spread_recv.at[d],
            device_id={"tm": lax.rem(tm + d, n_tm)},
            device_id_type=MESH,
        )

    def field_copy(step):
        slot = lax.rem(step, 2)
        return pltpu.make_async_remote_copy(
            src_ref=far_out.at[slot],
            dst_ref=far_in.at[step],
            send_sem=field_send.at[slot],
            recv_sem=field_recv.at[step],
            device_id={"space": partner},
            device_id_type=MESH,
        )

    def relay_copy(step):
        slot = lax.rem(step, 2)
        return pltpu.make_async_remote_copy(
            src_ref=outbox.at[slot, upper_half, pl.ds(0, 24), :],
            dst_ref=relay_in.at[step, pl.ds(0, 24), :],
            send_sem=relay_send.at[slot],
            recv_sem=relay_recv.at[step],
            device_id={"space": second},
            device_id_type=MESH,
        )

    def near(step, side):
        lower = has[0] & jnp.logical_not(across[0] & (step >= AHEAD))
        upper = has[1] & jnp.logical_not(across[1] & (step >= AHEAD))
        return ((side == 0) & lower) | ((side == 1) & upper)

    def fields_go(step):
        return (step >= AHEAD - 1) & (step < STEPS - 1)

    def store_twice(target, p, rows, value):
        half = lax.broadcasted_iota(jnp.int32, value.shape, 1) < BS
        turned = pltpu.roll(value, BS, 1)
        target[2 * p, rows, :] = jnp.where(half, value, turned)
        target[2 * p + 1, rows, :] = jnp.where(half, turned, value)

    def of_listed(blocks, q):
        values = [blocks[lists[upper_half, 2 * q + h]] for h in range(2)]
        return jnp.where(lax.broadcasted_iota(jnp.int32, values[0].shape, 1) < BS, *values)

    def arrive(step, p, value):
        begins = jnp.where(lax.rem(step, CF) == 0, 4 - C_DEV * tm - step // CF, -1)
        value = jnp.where(field == begins, start[pl.ds(p, 1), :], value)
        state[p] = value
        far_out[lax.rem(step, 2), pl.ds(4 * p, 4), :] = value[:4]
        doubled[2 * p], doubled[2 * p + 1] = twice(value)

    def send(step):
        slot = lax.rem(step, 2)

        @pl.when(is_far & fields_go(step))
        def _():
            field_copy(step).start()

        for side in (cross, 1 - cross):
            for q in range(HALO // 2):
                pair = jnp.where(low, doubled[lists[side, 2 * q]], doubled[lists[side, 2 * q + 1]])
                outbox[slot, side, pl.ds(3 * q, 3), :] = pair[:3]

            @pl.when(near(step, side))
            def _():
                halo_copy(slot, side).start()

        @pl.when(is_relay & fields_go(step))
        def _():
            relay_copy(step).start()

    @pl.when(is_far)
    def _():
        for load in loads:
            load.wait()
        for p in range(PAIRS):
            own_rows = pl.ds(pl.multiple_of(rows_each * tm, 8), rows_each)
            store_twice(block_rows, p, pl.ds(0, rows_each), coupling[own_rows, cells(p)])
        for q in range(HALO // 2):
            piece[:, cells(q)] = of_listed(block_rows, q)

    pl.semaphore_wait(
        barrier,
        4
        + has[0].astype(jnp.int32)
        + has[1].astype(jnp.int32)
        + (n_tm - 5) * is_far.astype(jnp.int32)
        + (is_far | is_relay).astype(jnp.int32),
    )


    for copy in slice_copies[:2]:
        copy.start()

    @pl.when(is_far)
    def _():
        far_copies[0].start()

    for copy in slice_copies[2:]:
        copy.start()
    for copy in slice_copies[:2]:
        copy.wait_recv()
    inputs[2].wait()
    for p in range(PAIRS):
        rows = [guess_in[pl.ds(16 * f + p, 1), :] for f in range(C_DEV)]
        rows.append(jnp.zeros((1, 128), jnp.float32))
        arrive(jnp.int32(0), p, jnp.concatenate(rows + rows, axis=0))
    send(jnp.int32(0))

    inputs[3].wait()
    inputs[4].wait()
    for p in range(PAIRS):
        retained[p] = jnp.where(top, retain[pl.ds(p, 1), :], 0.0)
    @pl.when(jnp.logical_not(is_far))
    def _():
        for load in loads:
            load.wait()

    for k in range(STENCIL):
        target, at, gap = (own_weights, 0, BS) if k == 0 else (weights, BS * (k - 1), REST)

        @pl.loop(0, BS // 16)
        def _(n, k=k, target=target, at=at, gap=gap):
            entries = coupling[pl.ds(pl.multiple_of(BS * k + 16 * n, 16), 16), :]
            upper = entries.astype(jnp.bfloat16)
            target[pl.ds(pl.multiple_of(at + 16 * n, 16), 16), :] = upper
            target[pl.ds(pl.multiple_of(at + gap + 16 * n, 16), 16), :] = (
                entries - upper.astype(jnp.float32)
            ).astype(jnp.bfloat16)

    def on_diagonal(product):
        return [
            jnp.where(
                low,
                product[16 * h : 16 * h + 8, 128 * h : 128 * h + 128],
                product[16 * h + 8 : 16 * h + 16, 128 * h : 128 * h + 128],
            )
            for h in range(2)
        ]

    def four_rows(value):
        return twice(in_parts(jnp.concatenate([value, value], axis=0)))

    def listed_by_partner(step):
        slot = lax.rem(step, 2)
        field_copy(step).wait_recv()
        relay_copy(step).wait_recv()
        for p in range(PAIRS):
            far_parts[2 * p], far_parts[2 * p + 1] = four_rows(far_in[step, pl.ds(4 * p, 4), :])
        for q in range(HALO // 2):
            at = NBLK + HALO * upper_half + 2 * q
            far_parts[at], far_parts[at + 1] = four_rows(relay_in[step, pl.ds(3 * q, 4), :])
            at = NBLK + HALO * (1 - upper_half) + 2 * q
            far_parts[at], far_parts[at + 1] = four_rows(outbox[slot, upper_half, pl.ds(3 * q, 4), :])
        begins = jnp.where(lax.rem(step + 1, CF) == 0, 4 - C_DEV * tm - (step + 1) // CF, -1)
        for g in range(HALO // 4):
            picked, firsts = [], []
            for j in range(4 * g, 4 * g + 4):
                firsts.append(far_parts[far_slots[j, STENCIL - 1]])
                rest = [
                    jnp.where(
                        low,
                        far_parts[far_slots[j, k]],
                        far_parts[far_slots[j, k + 1]],
                    )
                    for k in range(0, STENCIL - 1, 2)
                ]
                picked.append(jnp.concatenate(rest + rest + firsts[-1:], axis=1))
            product = jnp.dot(
                jnp.concatenate(picked, axis=0).astype(jnp.bfloat16),
                far_weights[:, 256 * g : 256 * g + 256],
                preferred_element_type=jnp.float32,
            )
            for h, pair in enumerate(on_diagonal(product)):
                q = 2 * g + h
                heat = far_forcing[pl.ds(step + 32 * q, 4, stride=CF), :]
                heat = jnp.concatenate([heat, jnp.zeros((4, 128), jnp.float32)], axis=0)
                now = jnp.where(low, firsts[2 * h], firsts[2 * h + 1])
                total = pair + far_cells[pl.ds(q, 1), :] * now + heat
                value = total + pltpu.roll(total, 4, 0)
                value = jnp.where(field == begins, far_cells[pl.ds(8 + q, 1), :], value)
                inbox[1 - slot, upper_half, pl.ds(3 * q, 3), :] = value[:3]

    def one_step(step, carry):
        slot = lax.rem(step, 2)

        @pl.when(step == 0)
        def _():
            for copy in slice_copies[2:]:
                copy.wait_recv()

        @pl.when((step == 0) & is_far)
        def _():
            for p in range(PAIRS):
                for a in range(8):
                    store_twice(block_forcing, p, pl.ds(4 * a, 4), forcing[pl.ds(64 * a + 4 * p, 4), :])
                for n, source in enumerate((retain, start)):
                    store_twice(block_cells, p, pl.ds(n, 1), source[pl.ds(p, 1), :])
            for q in range(HALO // 2):
                far_forcing_out[pl.ds(32 * q, 32), :] = of_listed(block_forcing, q)
                both = of_listed(block_cells, q)
                far_cells_out[pl.ds(q, 1), :] = both[0:1]
                far_cells_out[pl.ds(8 + q, 1), :] = both[1:2]
            wide = lax.broadcasted_iota(jnp.int32, (HALO, NBLK), 0)
            listed = jnp.zeros((HALO, NBLK), jnp.int32)
            for j in range(HALO):
                listed = jnp.where(wide == j, lists[upper_half, j], listed)
            chosen = listed == lax.broadcasted_iota(jnp.int32, (HALO, NBLK), 1)
            place_at = lax.broadcasted_iota(jnp.int32, (HALO, 128), 1)
            table = jnp.zeros((HALO, 128), jnp.int32)
            for k in range(STENCIL):
                if k < STENCIL - 1:
                    found = jnp.where(chosen, columns_own[pl.ds(k, 1), :], 0)
                else:
                    found = jnp.where(chosen, listed, 0)
                table = jnp.where(place_at == k, jnp.sum(found, axis=1, keepdims=True), table)
            far_slots_out[...] = table
            for copy in far_copies[1:]:
                copy.start()

        @pl.when((step == SPREAD) & is_far)
        def _():
            far_copies[0].wait_recv()
            for d in range(1, n_tm):
                spread_copy(d, tm).start()

        @pl.when((step == AHEAD - 1) & is_far)
        def _():
            for copy in far_copies[1:]:
                copy.wait_recv()
            slots = pltpu.make_async_copy(far_slots_in, far_slots, input_sem.at[7])
            slots.start()
            slots.wait()
            for d in range(1, n_tm):
                spread_copy(d, lax.rem(tm + n_tm - d, n_tm)).wait_recv()
            for k in range(STENCIL):
                at, gap = (2 * REST, BS) if k == 0 else (BS * (k - 1), REST)

                @pl.loop(0, BS // 16)
                def _(n, k=k, at=at, gap=gap):
                    entries = far_coupling[pl.ds(pl.multiple_of(BS * k + 16 * n, 16), 16), :]
                    upper = entries.astype(jnp.bfloat16)
                    far_weights[pl.ds(pl.multiple_of(at + 16 * n, 16), 16), :] = upper
                    far_weights[pl.ds(pl.multiple_of(at + gap + 16 * n, 16), 16), :] = (
                        entries - upper.astype(jnp.float32)
                    ).astype(jnp.bfloat16)

        @pl.when(step == 4 * CF)
        def _():
            for p in range(PAIRS):
                value = reached[p]
                values_out[pl.ds(0, 2), cells(p)] = value[1:3]
                point_out[pl.ds(p, 1), :] = value[0:1]
            point_copy.start()

        at = (step // CF) * 64 + lax.rem(step, CF)
        for g in range(GROUPS):
            own = []
            for b in range(4 * g, 4 * g + 4):
                own.append(in_parts(doubled[b]))
                parts[b] = own[-1]
            product = jnp.dot(
                jnp.concatenate(own, axis=0).astype(jnp.bfloat16),
                own_weights[:, 256 * g : 256 * g + 256],
                preferred_element_type=jnp.float32,
            )
            for h, pair in enumerate(on_diagonal(product)):
                p = 2 * g + h
                heat = forcing[pl.ds(at + 4 * p, 4, stride=64), :]
                heat = jnp.concatenate([heat, jnp.zeros((4, 128), jnp.float32)], axis=0)
                base[p] = pair + retained[p] * state[p] + heat

        for side in range(2):

            @pl.when(near(step, side))
            def _():
                halo_copy(slot, side).wait_send()

        @pl.when(is_far & fields_go(step))
        def _():
            field_copy(step).wait_send()

        @pl.when(is_relay & fields_go(step))
        def _():
            relay_copy(step).wait_send()

        @pl.when(is_far & (step >= AHEAD))
        def _():
            listed_by_partner(step - 1)

        for side in (1 - cross, cross):

            @pl.when(near(step, side))
            def _(side=side):
                halo_copy(slot, 1 - side).wait_recv()

            for q in range(HALO // 2):
                value = inbox[slot, side, pl.ds(3 * q, 4), :]
                n = NBLK + HALO * side + 2 * q
                parts[n], parts[n + 1] = four_rows(value)

        for g in range(GROUPS):
            picked = []
            for b in range(4 * g, 4 * g + 4):
                picked.append(
                    jnp.concatenate(
                        [
                            jnp.where(low, parts[columns[k, b]], parts[columns[k + 1, b]])
                            for k in range(0, STENCIL - 1, 2)
                        ],
                        axis=1,
                    )
                )
            left = jnp.concatenate(picked, axis=0).astype(jnp.bfloat16)
            product = jnp.dot(
                jnp.concatenate([left, left], axis=1),
                weights[:, 256 * g : 256 * g + 256],
                preferred_element_type=jnp.float32,
            )
            for h, pair in enumerate(on_diagonal(product)):
                total = base[2 * g + h] + pair
                value = total + pltpu.roll(total, 4, 0)
                reached[2 * g + h] = value
                arrive(step + 1, 2 * g + h, value)

        @pl.when(step < STEPS - 1)
        def _():
            send(step + 1)

        return carry

    lax.fori_loop(0, STEPS, one_step, 0)

    for copy in slice_copies:
        copy.wait_send()

    @pl.when(is_far)
    def _():
        for copy in far_copies:
            copy.wait_send()
        for d in range(1, n_tm):
            spread_copy(d, tm).wait_send()

    point_copy.wait()
    for p in range(PAIRS):
        values_out[pl.ds(2, 1), cells(p)] = point_in[pl.ds(p, 1), :]
        residual_out[:, cells(p)] = reached[p][:3] - values_out[:, cells(p)]


def body(n_tm, n_space, coupling, retain, sources, initial_guess, start_field, block_columns, send_lists):
    count = retain.shape[0]
    f32, bf16 = jnp.float32, jnp.bfloat16
    vmem = pl.BlockSpec(memory_space=pltpu.VMEM)
    return pl.pallas_call(
        functools.partial(kernel, n_tm, n_space),
        out_shape=(jax.ShapeDtypeStruct((C_DEV, count), f32),) * 2,
        in_specs=[pl.BlockSpec(memory_space=pl.ANY)] * 7,
        out_specs=(vmem, vmem),
        scratch_shapes=[
            pltpu.SMEM((STENCIL - 1, NBLK), jnp.int32),
            pltpu.SMEM((2, HALO), jnp.int32),
            pltpu.VMEM((PAIRS, 128), f32),
            pltpu.VMEM((C_DEV * CF, count), f32),
            pltpu.VMEM((C_DEV, count), f32),
            pltpu.VMEM((PAIRS, 128), f32),
            pltpu.VMEM((STENCIL * BS, count), f32),
            pltpu.VMEM((2 * BS, count), bf16),
            pltpu.VMEM((2 * REST, count), bf16),
            pltpu.VMEM((512, 128), f32),
            pltpu.VMEM((48, 128), f32),
            pltpu.VMEM((48, 128), f32),
            pltpu.VMEM((PAIRS, 8, 128), f32),
            pltpu.VMEM((PAIRS, 8, 128), f32),
            pltpu.VMEM((PAIRS, 8, 128), f32),
            pltpu.VMEM((NBLK, 8, 128), f32),
            pltpu.VMEM((NBLK + 2 * HALO, 8, 128), f32),
            pltpu.VMEM((PAIRS, 8, 128), f32),
            pltpu.VMEM((2, 2, 32, 128), f32),
            pltpu.VMEM((2, 2, 32, 128), f32),
            pltpu.VMEM((16, 128), f32),
            pltpu.VMEM((16, 128), f32),
            pltpu.VMEM((STENCIL * BS // n_tm, count // 2), f32),
            pltpu.VMEM((STENCIL * BS, count // 2), f32),
            pltpu.VMEM((2 * STENCIL * BS, count // 2), bf16),
            pltpu.VMEM((256, 128), f32),
            pltpu.VMEM((256, 128), f32),
            pltpu.VMEM((16, 128), f32),
            pltpu.VMEM((16, 128), f32),
            pltpu.VMEM((STENCIL - 1, NBLK), jnp.int32),
            pltpu.VMEM((HALO, 128), jnp.int32),
            pltpu.VMEM((HALO, 128), jnp.int32),
            pltpu.SMEM((HALO, 128), jnp.int32),
            pltpu.VMEM((NBLK, STENCIL * BS // n_tm, 128), f32),
            pltpu.VMEM((NBLK, 32, 128), f32),
            pltpu.VMEM((NBLK, 8, 128), f32),
            pltpu.VMEM((2, 64, 128), f32),
            pltpu.VMEM((STEPS, 64, 128), f32),
            pltpu.VMEM((STEPS, 32, 128), f32),
            pltpu.VMEM((NBLK + 2 * HALO, 8, 128), f32),
            pltpu.SemaphoreType.DMA((STENCIL,)),
            pltpu.SemaphoreType.DMA((8,)),
            pltpu.SemaphoreType.DMA((2, 2)),
            pltpu.SemaphoreType.DMA((2, 2)),
            pltpu.SemaphoreType.DMA((7,)),
            pltpu.SemaphoreType.DMA((7,)),
            pltpu.SemaphoreType.DMA((4,)),
            pltpu.SemaphoreType.DMA((4,)),
            pltpu.SemaphoreType.DMA((n_tm,)),
            pltpu.SemaphoreType.DMA((n_tm,)),
            pltpu.SemaphoreType.DMA((2,)),
            pltpu.SemaphoreType.DMA((STEPS,)),
            pltpu.SemaphoreType.DMA((2,)),
            pltpu.SemaphoreType.DMA((STEPS,)),
        ],
        compiler_params=pltpu.CompilerParams(
            collective_id=0, has_side_effects=True, vmem_limit_bytes=60 * 2**20
        ),
    )(
        send_lists,
        coupling,
        retain.reshape(PAIRS, 128),
        sources,
        initial_guess,
        start_field.reshape(PAIRS, 128),
        block_columns.T,
    )


def solution(mesh):
    placed = (
        P(None, "space"),
        P("space"),
        P("tm", "space"),
        P("tm", "space"),
        P("space"),
        P("space", None),
        P("space", None),
    )
    return jax.shard_map(
        functools.partial(body, mesh.shape["tm"], mesh.shape["space"]),
        mesh=mesh,
        in_specs=placed,
        out_specs=(P("tm", "space"), P("tm", "space")),
        check_vma=False,
    )
```
